512 devices in a mesh: sec: 2 (over y_hi), slab: 64 (over x, z), col: 4 (over y_lo, core).
Axes of the slice: x: 4, y: 4 (y_hi: 2, y_lo: 2; y = y_hi * 2 + y_lo), z: 16, core: 2. Of those that a mesh axis runs over, the one named last changes fastest.
Arguments:
- volume: float32 [2, 20, 512, 32, 256], P('sec', None, 'slab', 'col'), may hold values from -4 to 4, as said below
- epi_line: int32 [64, 4, 64], P('slab', 'col'), may hold values from 0 to 63
- epi_dest: int32 [64, 4, 64, 1], P('slab', 'col'), may hold values from 0 to 63, as said below
- epi_target: int32 [64, 4, 64], P('slab', 'col'), may hold values from 0 to 319
Outputs:
- volume_next: float32 [2, 20, 512, 32, 256], P('sec', None, 'slab', 'col')
The draws below stay inside these ranges and needn't reach their ends.
Inputs may be any that keep to these rules, and one draw needn't show every extreme that they name: `epi_dest`: in each heart block of 64 rows (slab s, one col) every named torso slab is named by exactly 2 rows. `volume`: gates lie in (0, 1); conductivities and reaction terms are positive.
All inputs are finite; a program needn't handle non-finite values.
Results may differ from the reference program's by a relative error of at most 0.0001.
Values sent between devices are 32-bit elements; how exact they have to be, the bound alone decides.
A program may use at most 64 MiB of HBM per device.

```python
import jax
import jax.numpy as jnp
import numpy as np

CX = 8
CY = 8
STEPS = 4
CAP = 2
EPI = 64
NX = 512
NY = 32
NZ = 256
N_SLAB = 64
N_COL = 4


def draw_volume(key, part):
    key = jax.random.fold_in(key, 11)
    keys = jax.random.split(key, 6)
    grid = (NX, NY, NZ)
    volts = jnp.clip(jax.random.normal(keys[0], (1,) + grid, jnp.float32), -4.0, 4.0)
    torso_pot = jnp.clip(0.5 * jax.random.normal(keys[3], (10,) + grid, jnp.float32), -4.0, 4.0)
    source = jnp.clip(jax.random.normal(keys[5], (5,) + grid, jnp.float32), -4.0, 4.0)
    gates = jax.random.uniform(keys[1], (18,) + grid, jnp.float32, 0.02, 0.98)
    sigma = jnp.exp(jax.random.uniform(keys[2], (1,) + grid, jnp.float32, -0.693, 0.693))
    mass_term = jnp.exp(jax.random.uniform(keys[4], (5,) + grid, jnp.float32, -1.386, 0.693))
    heart = jnp.concatenate([volts, gates, sigma], axis=0)
    torso = jnp.concatenate([torso_pot, mass_term, source], axis=0)
    return jnp.stack([heart, torso], axis=0)


def block_routes(block_key, slab_number):
    first_key, second_key = jax.random.split(block_key, 2)
    others = jax.random.permutation(first_key, N_SLAB - 1).astype(jnp.int32) + 1
    offsets = jnp.concatenate([jnp.zeros((1,), jnp.int32), others], axis=0)
    order = jax.random.permutation(second_key, EPI).astype(jnp.int32)
    group = order // CAP
    return (slab_number + 1 + offsets[group]) % N_SLAB


def draw_epi_dest(key, part):
    key = jax.random.fold_in(key, 23)
    keys = jax.random.split(key, N_SLAB * N_COL)
    slab_numbers = jnp.repeat(jnp.arange(N_SLAB, dtype=jnp.int32), N_COL)
    routed = jax.vmap(block_routes)(keys, slab_numbers)
    return routed.reshape(N_SLAB, N_COL, EPI, 1).astype(jnp.int32)


def touch_ends(entries, own_key, low, top_value):
    extent = entries.shape
    place = [jax.random.randint(jax.random.fold_in(own_key, axis), (), 0, extent[axis]) for axis in range(len(extent))]
    entries = entries.at[tuple(place)].set(low)
    longest = extent.index(max(extent))
    place[longest] = (place[longest] + 1) % extent[longest]
    return entries.at[tuple(place)].set(top_value)


def setup_inputs(seed: int = 0) -> dict:
    seeds = jax.random.split(jax.random.key(seed), 5)
    volume = draw_volume(jax.random.fold_in(seeds[4], 71), 0)
    epi_line = touch_ends(jax.random.randint(seeds[1], (N_SLAB, N_COL, EPI), 0, CX * CY), jax.random.fold_in(seeds[1], 1), 0, (CX * CY) - 1).astype(jnp.int32)
    epi_dest = draw_epi_dest(jax.random.fold_in(seeds[4], 71), 0)
    epi_target = touch_ends(jax.random.randint(seeds[3], (N_SLAB, N_COL, EPI), 0, 5 * CX * CY), jax.random.fold_in(seeds[3], 1), 0, (5 * CX * CY) - 1).astype(jnp.int32)
    return dict(volume=volume, epi_line=epi_line, epi_dest=epi_dest, epi_target=epi_target)


gate_half = np.linspace(-1.5, 1.5, 18).reshape(18, 1, 1, 1).astype(np.float32)
gate_slope = (0.3 + 0.1 * (np.arange(18) % 4)).reshape(18, 1, 1, 1).astype(np.float32)
gate_decay = np.exp(-1.0 / (2.0 * 30.0 ** (np.arange(18) / 17.0))).reshape(18, 1, 1, 1).astype(np.float32)
gate_conduct = (0.02 + 0.01 * (np.arange(18) % 3)).reshape(18, 1, 1, 1).astype(np.float32)
gate_reversal = np.linspace(-1.0, 1.0, 18).reshape(18, 1, 1, 1).astype(np.float32)
relax_omega = 1.5625


def ionic(volts, gates, sigma, lap_x, lap_y, lap_z):
    steady = jax.nn.sigmoid((volts[None] - gate_half) / gate_slope)
    gates = steady + (gates - steady) * gate_decay
    current = jnp.sum(gate_conduct * gates * (volts[None] - gate_reversal), axis=0)
    volts = volts + sigma * (0.12 * lap_x + 0.04 * lap_y + 0.04 * lap_z) - current
    return volts, gates


def heart_step(heart):
    volts = heart[0]
    padded = jnp.pad(volts, 1, mode="edge")
    lap_x = padded[2:, 1:-1, 1:-1] + padded[:-2, 1:-1, 1:-1] - 2.0 * volts
    lap_y = padded[1:-1, 2:, 1:-1] + padded[1:-1, :-2, 1:-1] - 2.0 * volts
    lap_z = padded[1:-1, 1:-1, 2:] + padded[1:-1, 1:-1, :-2] - 2.0 * volts
    volts, gates = ionic(volts, heart[1:19], heart[19], lap_x, lap_y, lap_z)
    return jnp.concatenate([volts[None], gates, heart[19:]], axis=0)


def torso_sweep(potential, previous, mass_term, source):
    padded = jnp.pad(potential, 1)
    beside = padded[2:, 1:-1, 1:-1] + padded[:-2, 1:-1, 1:-1]
    beside = beside + padded[1:-1, 2:, 1:-1] + padded[1:-1, :-2, 1:-1]
    beside = beside + padded[1:-1, 1:-1, 2:] + padded[1:-1, 1:-1, :-2]
    applied = (6.0 + mass_term) * potential - beside
    update = (source - applied) / (6.0 + mass_term)
    fresh = previous + relax_omega * (potential + update - previous)
    return fresh, potential


def to_torso(section):
    segmented = section.reshape(4, 5, N_SLAB, CX, NY, NZ).transpose(0, 2, 1, 3, 4, 5)
    return segmented.reshape(4, 5 * NX, NY, NZ)


def from_torso(fields):
    segmented = fields.reshape(4, N_SLAB, 5, CX, NY, NZ).transpose(0, 2, 1, 3, 4, 5)
    return segmented.reshape(20, NX, NY, NZ)


def reference(volume, epi_line, epi_dest, epi_target):
    heart = volume[0]
    torso = to_torso(volume[1])
    potential, previous, mass_term = torso[0], torso[1], torso[2]
    source = torso[3]
    for step in range(STEPS):
        heart = heart_step(heart)
        potential, previous = torso_sweep(potential, previous, mass_term, source)
    slab_ids = jnp.arange(N_SLAB, dtype=jnp.int32)[:, None, None]
    col_ids = jnp.arange(N_COL, dtype=jnp.int32)[None, :, None]
    heart_x = slab_ids * CX + epi_line // CY
    heart_y = col_ids * CY + epi_line % CY
    values = heart[0][heart_x, heart_y]
    dest = epi_dest[..., 0]
    torso_x = dest * (5 * CX) + epi_target // CY
    torso_y = col_ids * CY + epi_target % CY
    inflow = jnp.zeros((5 * NX, NY, NZ), jnp.float32).at[torso_x, torso_y].add(values)
    torso_out = from_torso(jnp.stack([potential, previous, mass_term, inflow], axis=0))
    return jnp.stack([heart, torso_out], axis=0)
```

```python
import functools

import jax
import jax.numpy as jnp
import numpy as np
from jax import lax
from jax.experimental import pallas as pl
from jax.experimental.pallas import tpu as pltpu
from jax.sharding import PartitionSpec as P

STEPS = 4
CAP = 2
GATES = 18
LANES = 128
SEGMENTS = 5
MESH = pl.DeviceIdType.MESH

gate_half = np.linspace(-1.5, 1.5, GATES)
gate_slope = 0.3 + 0.1 * (np.arange(GATES) % 4)
gate_decay = np.exp(-1.0 / (2.0 * 30.0 ** (np.arange(GATES) / 17.0)))
gate_conduct = 0.02 + 0.01 * (np.arange(GATES) % 3)
gate_reversal = np.linspace(-1.0, 1.0, GATES)
relax_omega = 1.5625


def iota(shape, dim):
    return lax.broadcasted_iota(jnp.int32, shape, dim)


def split_halves(x):
    high = x.astype(jnp.bfloat16)
    low = (x - high.astype(jnp.float32)).astype(jnp.bfloat16)
    return jnp.concatenate([high, low], axis=0)


def matmul(a, b, contract):
    return lax.dot_general(
        a, b, (contract, ((), ())), preferred_element_type=jnp.float32
    )


def kernel(
    n_slab, n_col,
    vol, line_hbm, dest_hbm, target_hbm, out,
    pots, coef, coef_src, faces, halo_x, halo_y,
    picks, rows_out, rows_in, lines_out, lines_in, meta,
    load_sem, meta_sem, send_sem, recv_sem, row_sem, line_sem,
):
    sec = lax.axis_index("sec")
    slab = lax.axis_index("slab")
    col = lax.axis_index("col")
    slab_low, slab_high = lax.rem(slab + n_slab - 1, n_slab), lax.rem(slab + 1, n_slab)
    col_low, col_high = lax.rem(col + n_col - 1, n_col), lax.rem(col + 1, n_col)
    nx, ny, nz = vol.shape[2], vol.shape[3], vol.shape[4]
    tx = SEGMENTS * nx
    plane = (ny, nz)
    sub, lane = iota(plane, 0), iota(plane, 1)
    low_y = jnp.logical_and(sub == 0, col > 0)
    high_y = jnp.logical_and(sub == ny - 1, col < n_col - 1)

    def load(index, src, dst):
        copy = pltpu.make_async_copy(src, dst, load_sem.at[index])
        copy.start()
        return copy

    barrier = pltpu.get_barrier_semaphore()
    neighbours = (
        (sec, slab_low, col), (sec, slab_high, col), (sec, slab, col_low), (sec, slab, col_high),
    )

    def greet():
        for there in neighbours:
            pl.semaphore_signal(barrier, inc=1, device_id=there, device_id_type=MESH)

    def exchange(step, first, last, width):
        return [
            pltpu.make_async_remote_copy(
                src_ref=src, dst_ref=dst, send_sem=send_sem.at[step, way],
                recv_sem=recv_sem.at[step, way], device_id=neighbours[way], device_id_type=MESH,
            )
            for way, (src, dst) in enumerate(
                (
                    (first, halo_x.at[step, 1]),
                    (last, halo_x.at[step, 0]),
                    (faces.at[step, 0, pl.ds(0, width)], halo_y.at[step, 1, pl.ds(0, width)]),
                    (faces.at[step, 1, pl.ds(0, width)], halo_y.at[step, 0, pl.ds(0, width)]),
                )
            )
        ]

    def to_all(src, dst, sems):
        def send(i, _):
            there = lax.rem(slab + i, n_slab)
            pltpu.make_async_remote_copy(
                src_ref=src.at[there], dst_ref=dst.at[slab], send_sem=sems.at[0],
                recv_sem=sems.at[1], device_id=(1, there, col), device_id_type=MESH,
            ).start()
            return 0

        lax.fori_loop(0, n_slab, send, 0)

    def wait_whole(ref, sem):
        pltpu.make_async_copy(ref, ref, sem).wait()

    def heart():
        loads = [
            load(0, vol.at[0, 0], pots.at[0, 0]),
            load(1, vol.at[0, pl.ds(1, GATES + 1)], out.at[0, pl.ds(1, GATES + 1)]),
        ]
        metas = [
            pltpu.make_async_copy(src.at[0], meta.at[i], meta_sem.at[i])
            for i, src in enumerate((line_hbm, dest_hbm, target_hbm))
        ]
        for copy in metas:
            copy.start()
        greet()

        for copy in metas:
            copy.wait()
        epi = meta.shape[2]
        line, dest, target = meta[0], meta[1], meta[2]
        slots = 4 * n_slab
        own = iota((slots, epi), 0)
        marks = own // 4 == dest
        before = (iota((epi, epi), 0) < iota((epi, epi), 1)).astype(jnp.bfloat16)
        rank = matmul(marks.astype(jnp.float32).astype(jnp.bfloat16), before, ((1,), (0,)))
        wanted = ((own // 2) % 2).astype(jnp.float32)
        place = jnp.logical_and(marks, rank == wanted)
        half = (own % 2).astype(jnp.float32)
        place = place.astype(jnp.float32)
        places = jnp.concatenate([place * (1.0 - half), place * half], axis=1)
        lines = nx * ny
        held = (iota((lines, epi), 0) == line).astype(jnp.float32).astype(jnp.bfloat16)
        for h in range(2):
            part = matmul(
                places[:, h * epi : (h + 1) * epi].astype(jnp.bfloat16), held, ((1,), (1,))
            ).astype(jnp.bfloat16)
            picks[:, h * lines : (h + 1) * lines] = part
            picks[:, (h + 2) * lines : (h + 3) * lines] = part
        own_d = iota((n_slab, epi), 0)
        marks_d = own_d == dest
        rank_d = matmul(marks_d.astype(jnp.float32).astype(jnp.bfloat16), before, ((1,), (0,)))
        goals = []
        for r in range(CAP):
            chosen = jnp.logical_and(marks_d, rank_d == float(r))
            goal = jnp.where(chosen, (target + 1).astype(jnp.float32), 0.0)
            goals.append(jnp.sum(goal, axis=1, keepdims=True) - 1.0)
        lane_s = iota((n_slab, LANES), 1)
        lines_out[:, 0, :] = jnp.where(lane_s < n_slab, goals[0], goals[1])

        loads[0].wait()
        for face, row in enumerate((0, ny - 1)):
            for x in range(nx):
                faces[0, face, x : x + 1, :] = pots[0, 0, x, row : row + 1, :]
        pl.semaphore_wait(barrier, 4 + n_slab)
        sends = exchange(0, pots.at[0, 0, 0], pots.at[0, 0, nx - 1], nx)
        for copy in sends:
            copy.start()
        to_all(lines_out, lines_in, line_sem)
        loads[1].wait()

        started = list(sends)
        for step in range(STEPS):

            def inner(x, _):
                volts = pots[step, 0, x]
                sigma = out[0, GATES + 1, x]
                beside_x = pots[step, 0, jnp.maximum(x - 1, 0)]
                beside_x += pots[step, 0, jnp.minimum(x + 1, nx - 1)]
                beside = jnp.where(sub == 0, volts, pltpu.roll(volts, 1, 0))
                beside += jnp.where(sub == ny - 1, volts, pltpu.roll(volts, ny - 1, 0))
                beside += jnp.where(lane == 0, volts, pltpu.roll(volts, 1, 1))
                beside += jnp.where(lane == nz - 1, volts, pltpu.roll(volts, nz - 1, 1))
                flux = 0.12 * (beside_x - 2.0 * volts) + 0.04 * (beside - 4.0 * volts)
                scaled = {}
                sums, weighted = {}, {}
                for j in range(GATES):
                    slope = float(0.5 / gate_slope[j])
                    if slope not in scaled:
                        scaled[slope] = volts * slope
                    bend = jnp.tanh(scaled[slope] - float(gate_half[j] * slope))
                    rest = float(0.5 * (1.0 - gate_decay[j]))
                    gate = out[0, 1 + j, x] * float(gate_decay[j]) + (rest * bend + rest)
                    out[0, 1 + j, x] = gate
                    conduct = float(gate_conduct[j])
                    drawn = gate * float(gate_reversal[j])
                    if conduct in sums:
                        sums[conduct] += gate
                        weighted[conduct] += drawn
                    else:
                        sums[conduct], weighted[conduct] = gate, drawn
                current = sum(c * (volts * sums[c] - weighted[c]) for c in sums)
                pots[step + 1, 0, x] = volts + sigma * flux - current
                return 0

            lax.fori_loop(0, nx, inner, 0)
            for copy in sends:
                copy.wait_recv()
            for x, here, there in ((0, slab > 0, 0), (nx - 1, slab < n_slab - 1, 1)):
                gain = jnp.where(here, 0.12, 0.0)
                pots[step + 1, 0, x] += gain * out[0, GATES + 1, x] * (
                    halo_x[step, there] - pots[step, 0, x]
                )

            for x in range(nx):
                volts = pots[step, 0, x]
                beyond = jnp.where(low_y, halo_y[step, 0, x : x + 1, :] - volts, 0.0)
                beyond += jnp.where(high_y, halo_y[step, 1, x : x + 1, :] - volts, 0.0)
                fresh = pots[step + 1, 0, x] + 0.04 * out[0, GATES + 1, x] * beyond
                pots[step + 1, 0, x] = fresh
                if step + 1 < STEPS:
                    faces[step + 1, 0, x : x + 1, :] = fresh[:1]
                    faces[step + 1, 1, x : x + 1, :] = fresh[ny - 1 :]
                else:
                    out[0, 0, x] = fresh
            if step + 1 < STEPS:
                sends = exchange(step + 1, pots.at[step + 1, 0, 0], pots.at[step + 1, 0, nx - 1], nx)
                for copy in sends:
                    copy.start()
                started += sends

        final = pots[STEPS, 0].reshape(lines, nz)
        source = jnp.concatenate([final[:, :LANES], final[:, LANES:]], axis=0)
        rows = matmul(picks[...], split_halves(source), ((1,), (0,)))
        rows_out[...] = rows.reshape(n_slab, 4, LANES)
        to_all(rows_out, rows_in, row_sem)
        for copy in started:
            copy.wait_send()
        wait_whole(lines_out, line_sem.at[0])
        wait_whole(rows_out, row_sem.at[0])

    def torso():
        def field(ref, f):
            return ref.at[0, pl.ds(SEGMENTS * f, SEGMENTS)]

        loads = [
            load(0, field(vol, 0), pots.at[0]),
            load(1, field(vol, 2), field(out, 2)),
            load(2, field(vol, 3), coef_src),
            load(3, field(vol, 1), field(out, 1)),
        ]
        greet()

        def invite(i, _):
            pl.semaphore_signal(
                barrier, inc=1, device_id=(0, lax.rem(slab + i, n_slab), col), device_id_type=MESH
            )
            return 0

        lax.fori_loop(0, n_slab, invite, 0)
        loads[0].wait()
        for face, row in enumerate((0, ny - 1)):
            for x in range(tx):
                faces[0, face, x : x + 1, :] = pots[0, x // nx, x % nx, row : row + 1, :]
        pl.semaphore_wait(barrier, 4)
        sends = exchange(0, pots.at[0, 0, 0], pots.at[0, SEGMENTS - 1, nx - 1], tx)
        for copy in sends:
            copy.start()
        for copy in loads[1:]:
            copy.wait()

        started = list(sends)
        mass = field(out, 2)
        for step in range(STEPS):
            now = pots.at[step]
            fresh_ref = pots.at[step + 1]
            before = pots.at[step - 1] if step else field(out, 1)

            def inner(k, _):
                planes = [now[k, r] for r in range(nx)]
                below = jnp.where(k > 0, now[jnp.maximum(k - 1, 0), nx - 1], 0.0)
                above = jnp.where(k < SEGMENTS - 1, now[jnp.minimum(k + 1, SEGMENTS - 1), 0], 0.0)
                around = [below] + planes + [above]
                for r in range(nx):
                    here = planes[r]
                    beside = around[r] + around[r + 2]
                    beside += jnp.where(sub == 0, 0.0, pltpu.roll(here, 1, 0))
                    beside += jnp.where(sub == ny - 1, 0.0, pltpu.roll(here, ny - 1, 0))
                    beside += jnp.where(lane == 0, 0.0, pltpu.roll(here, 1, 1))
                    beside += jnp.where(lane == nz - 1, 0.0, pltpu.roll(here, nz - 1, 1))
                    if step == 0:
                        gain = relax_omega / (6.0 + mass[k, r])
                        drive = gain * coef_src[k, r]
                        coef[k, r] = gain
                        coef_src[k, r] = drive
                    else:
                        gain = coef[k, r]
                        drive = coef_src[k, r]
                    fresh_ref[k, r] = (
                        drive + (1.0 - relax_omega) * before[k, r] + gain * beside
                    )
                return 0

            lax.fori_loop(0, SEGMENTS, inner, 0)
            for copy in sends:
                copy.wait_recv()
            for k, r, here, there in (
                (0, 0, slab > 0, 0), (SEGMENTS - 1, nx - 1, slab < n_slab - 1, 1),
            ):
                fresh_ref[k, r] += jnp.where(here, 1.0, 0.0) * coef[k, r] * halo_x[step, there]

            def outer(k, _):
                base = k * nx
                low = halo_y[step, 0, pl.ds(base, nx), :]
                high = halo_y[step, 1, pl.ds(base, nx), :]
                for r in range(nx):
                    beyond = jnp.where(low_y, low[r : r + 1], 0.0)
                    beyond += jnp.where(high_y, high[r : r + 1], 0.0)
                    fresh = fresh_ref[k, r] + coef[k, r] * beyond
                    fresh_ref[k, r] = fresh
                    if step + 1 < STEPS:
                        faces[step + 1, 0, pl.ds(base + r, 1), :] = fresh[:1]
                        faces[step + 1, 1, pl.ds(base + r, 1), :] = fresh[ny - 1 :]
                    if step + 2 == STEPS:
                        out[0, SEGMENTS + k, r] = fresh
                    if step + 1 == STEPS:
                        out[0, k, r] = fresh
                return 0

            lax.fori_loop(0, SEGMENTS, outer, 0)
            if step + 1 < STEPS:
                sends = exchange(
                    step + 1, fresh_ref.at[0, 0], fresh_ref.at[SEGMENTS - 1, nx - 1], tx
                )
                for copy in sends:
                    copy.start()
                started += sends

        wait_whole(lines_in, line_sem.at[1])
        marks = jnp.where(
            iota((n_slab, LANES), 0) == iota((n_slab, LANES), 1) % n_slab, lines_in[:, 0, :], 0.0
        )
        marks = jnp.sum(marks, axis=0, keepdims=True)[:, : CAP * n_slab]
        goals = iota((tx * ny, CAP * n_slab), 0).astype(jnp.float32)
        hits = (goals == marks).astype(jnp.float32).astype(jnp.bfloat16)
        wait_whole(rows_in, row_sem.at[1])
        got = jnp.concatenate(
            [
                jnp.concatenate([rows_in[:, 2 * r + h, :] for r in range(CAP)], axis=0)
                for h in range(2)
            ],
            axis=1,
        )
        inflow = matmul(jnp.concatenate([hits, hits], axis=1), split_halves(got), ((1,), (0,)))
        out[0, pl.ds(3 * SEGMENTS, SEGMENTS)] = inflow.reshape(SEGMENTS, nx, ny, nz)
        for copy in started:
            copy.wait_send()

    pl.when(sec == 0)(heart)
    pl.when(sec == 1)(torso)


def solution(mesh):
    n_slab, n_col = mesh.shape["slab"], mesh.shape["col"]

    def on_device(volume, epi_line, epi_dest, epi_target):
        _, fields, nx, ny, nz = volume.shape
        epi = epi_line.shape[-1]
        tx = SEGMENTS * nx
        f32 = jnp.float32
        return pl.pallas_call(
            functools.partial(kernel, n_slab, n_col),
            out_shape=jax.ShapeDtypeStruct(volume.shape, f32),
            in_specs=[pl.BlockSpec(memory_space=pl.ANY)] * 4,
            out_specs=pl.BlockSpec(memory_space=pltpu.VMEM),
            scratch_shapes=[
                pltpu.VMEM((STEPS + 1, SEGMENTS, nx, ny, nz), f32),
                pltpu.VMEM((SEGMENTS, nx, ny, nz), f32),
                pltpu.VMEM((SEGMENTS, nx, ny, nz), f32),
                pltpu.VMEM((STEPS, 2, tx, nz), f32),
                pltpu.VMEM((STEPS, 2, ny, nz), f32),
                pltpu.VMEM((STEPS, 2, tx, nz), f32),
                pltpu.VMEM((4 * n_slab, 4 * nx * ny), jnp.bfloat16),
                pltpu.VMEM((n_slab, 4, LANES), f32),
                pltpu.VMEM((n_slab, 4, LANES), f32),
                pltpu.VMEM((n_slab, 1, LANES), f32),
                pltpu.VMEM((n_slab, 1, LANES), f32),
                pltpu.VMEM((3, 1, epi), jnp.int32),
                pltpu.SemaphoreType.DMA((4,)),
                pltpu.SemaphoreType.DMA((3,)),
                pltpu.SemaphoreType.DMA((STEPS, 4)),
                pltpu.SemaphoreType.DMA((STEPS, 4)),
                pltpu.SemaphoreType.DMA((2,)),
                pltpu.SemaphoreType.DMA((2,)),
            ],
            compiler_params=pltpu.CompilerParams(
                collective_id=0, has_side_effects=True, vmem_limit_bytes=24 * 1024 * 1024
            ),
        )(volume, epi_line, epi_dest.reshape(epi_line.shape), epi_target)

    return jax.shard_map(
        on_device,
        mesh=mesh,
        in_specs=(
            P("sec", None, "slab", "col", None),
            P("slab", "col", None),
            P("slab", "col", None, None),
            P("slab", "col", None),
        ),
        out_specs=P("sec", None, "slab", "col", None),
        check_vma=False,
    )
```

```python
import functools

import jax
import jax.numpy as jnp
import numpy as np
from jax import lax
from jax.experimental import pallas as pl
from jax.experimental.pallas import tpu as pltpu
from jax.sharding import PartitionSpec as P

STEPS = 4
CAP = 2
GATES = 18
LANES = 128
SEGMENTS = 5
VMEM_LIMIT = 24 * 1024 * 1024
MESH = pl.DeviceIdType.MESH

gate_half = np.linspace(-1.5, 1.5, GATES)
gate_slope = 0.3 + 0.1 * (np.arange(GATES) % 4)
gate_decay = np.exp(-1.0 / (2.0 * 30.0 ** (np.arange(GATES) / 17.0)))
gate_conduct = 0.02 + 0.01 * (np.arange(GATES) % 3)
gate_reversal = np.linspace(-1.0, 1.0, GATES)
relax_omega = 1.5625


def iota(shape, dim):
    return lax.broadcasted_iota(jnp.int32, shape, dim)


def split_halves(x):
    high = x.astype(jnp.bfloat16)
    low = (x - high.astype(jnp.float32)).astype(jnp.bfloat16)
    return jnp.concatenate([high, low], axis=0)


def matmul(a, b, contract):
    return lax.dot_general(
        a, b, (contract, ((), ())), preferred_element_type=jnp.float32
    )


class Place:
    def __init__(self, n_slab, n_col, sizes):
        self.n_slab, self.n_col = n_slab, n_col
        self.sec = sec = lax.axis_index("sec")
        self.slab = slab = lax.axis_index("slab")
        self.col = col = lax.axis_index("col")
        slab_low, slab_high = lax.rem(slab + n_slab - 1, n_slab), lax.rem(slab + 1, n_slab)
        col_low, col_high = lax.rem(col + n_col - 1, n_col), lax.rem(col + 1, n_col)
        self.neighbours = (
            (sec, slab_low, col), (sec, slab_high, col),
            (sec, slab, col_low), (sec, slab, col_high),
        )
        _, _, _, ny, nz = sizes
        self.sub, self.lane = iota((ny, nz), 0), iota((ny, nz), 1)
        self.low_y = jnp.logical_and(self.sub == 0, col > 0)
        self.high_y = jnp.logical_and(self.sub == ny - 1, col < n_col - 1)

    def greet(self):
        for there in self.neighbours:
            pl.semaphore_signal(
                pltpu.get_barrier_semaphore(), inc=1, device_id=there, device_id_type=MESH
            )

    def exchange(self, step, first, last, faces, halo_x, halo_y, send_sem, recv_sem):
        pairs = (
            (first, halo_x.at[step, 1]),
            (last, halo_x.at[step, 0]),
            (faces.at[step, 0], halo_y.at[step, 1]),
            (faces.at[step, 1], halo_y.at[step, 0]),
        )
        return [
            pltpu.make_async_remote_copy(
                src_ref=src, dst_ref=dst, send_sem=send_sem.at[step, way],
                recv_sem=recv_sem.at[step, way], device_id=self.neighbours[way],
                device_id_type=MESH,
            )
            for way, (src, dst) in enumerate(pairs)
        ]


def load(src, dst, sem):
    copy = pltpu.make_async_copy(src, dst, sem)
    copy.start()
    return copy


def wait_whole(ref, sem):
    pltpu.make_async_copy(ref, ref, sem).wait()


def heart_kernel(
    n_slab, n_col,
    vol, line_hbm, dest_hbm, target_hbm, state, rows_out,
    pots, faces, halo_x, halo_y, picks, meta,
    load_sem, meta_sem, send_sem, recv_sem,
):
    place_ = Place(n_slab, n_col, vol.shape)
    slab, sub, lane = place_.slab, place_.sub, place_.lane
    low_y, high_y = place_.low_y, place_.high_y
    nx, ny, nz = vol.shape[2:]

    def heart():
        loads = [
            load(vol.at[0, 0], pots.at[0], load_sem.at[0]),
            load(vol.at[0, pl.ds(1, GATES + 1)], state.at[pl.ds(1, GATES + 1)], load_sem.at[1]),
        ]
        metas = [
            pltpu.make_async_copy(src.at[0], meta.at[i], meta_sem.at[i])
            for i, src in enumerate((line_hbm, dest_hbm, target_hbm))
        ]
        for copy in metas:
            copy.start()
        place_.greet()

        for copy in metas:
            copy.wait()
        epi = meta.shape[2]
        line, dest, target = meta[0], meta[1], meta[2]
        slots = 4 * n_slab
        own = iota((slots, epi), 0)
        marks = own // 4 == dest
        before = (iota((epi, epi), 0) < iota((epi, epi), 1)).astype(jnp.bfloat16)
        rank = matmul(marks.astype(jnp.float32).astype(jnp.bfloat16), before, ((1,), (0,)))
        wanted = ((own // 2) % 2).astype(jnp.float32)
        place = jnp.logical_and(marks, rank == wanted)
        half = (own % 2).astype(jnp.float32)
        place = place.astype(jnp.float32)
        places = jnp.concatenate([place * (1.0 - half), place * half], axis=1)
        lines = nx * ny
        held = (iota((lines, epi), 0) == line).astype(jnp.float32).astype(jnp.bfloat16)
        for h in range(2):
            part = matmul(
                places[:, h * epi : (h + 1) * epi].astype(jnp.bfloat16), held, ((1,), (1,))
            ).astype(jnp.bfloat16)
            picks[:, h * lines : (h + 1) * lines] = part
            picks[:, (h + 2) * lines : (h + 3) * lines] = part
        own_d = iota((n_slab, epi), 0)
        marks_d = own_d == dest
        rank_d = matmul(marks_d.astype(jnp.float32).astype(jnp.bfloat16), before, ((1,), (0,)))
        goals = []
        for r in range(CAP):
            chosen = jnp.logical_and(marks_d, rank_d == float(r))
            goal = jnp.where(chosen, (target + 1).astype(jnp.float32), 0.0)
            goals.append(jnp.sum(goal, axis=1, keepdims=True) - 1.0)
        lane_s = iota((n_slab, LANES), 1)
        rows_out[:, 4, :] = jnp.where(lane_s < n_slab, goals[0], goals[1])

        loads[0].wait()
        for face, row in enumerate((0, ny - 1)):
            for x in range(nx):
                faces[0, face, x : x + 1, :] = pots[0, x, row : row + 1, :]
        pl.semaphore_wait(pltpu.get_barrier_semaphore(), 4)
        links = (faces, halo_x, halo_y, send_sem, recv_sem)
        sends = place_.exchange(0, pots.at[0, 0], pots.at[0, nx - 1], *links)
        for copy in sends:
            copy.start()
        loads[1].wait()

        started = list(sends)
        for step in range(STEPS):

            def inner(x, _):
                volts = pots[step, x]
                sigma = state[GATES + 1, x]
                beside_x = pots[step, jnp.maximum(x - 1, 0)]
                beside_x += pots[step, jnp.minimum(x + 1, nx - 1)]
                beside = jnp.where(sub == 0, volts, pltpu.roll(volts, 1, 0))
                beside += jnp.where(sub == ny - 1, volts, pltpu.roll(volts, ny - 1, 0))
                beside += jnp.where(lane == 0, volts, pltpu.roll(volts, 1, 1))
                beside += jnp.where(lane == nz - 1, volts, pltpu.roll(volts, nz - 1, 1))
                flux = 0.12 * (beside_x - 2.0 * volts) + 0.04 * (beside - 4.0 * volts)
                scaled = {}
                sums, weighted = {}, {}
                for j in range(GATES):
                    slope = float(0.5 / gate_slope[j])
                    if slope not in scaled:
                        scaled[slope] = volts * slope
                    bend = jnp.tanh(scaled[slope] - float(gate_half[j] * slope))
                    rest = float(0.5 * (1.0 - gate_decay[j]))
                    gate = state[1 + j, x] * float(gate_decay[j]) + (rest * bend + rest)
                    state[1 + j, x] = gate
                    conduct = float(gate_conduct[j])
                    drawn = gate * float(gate_reversal[j])
                    if conduct in sums:
                        sums[conduct] += gate
                        weighted[conduct] += drawn
                    else:
                        sums[conduct], weighted[conduct] = gate, drawn
                current = sum(c * (volts * sums[c] - weighted[c]) for c in sums)
                pots[step + 1, x] = volts + sigma * flux - current
                return 0

            lax.fori_loop(0, nx, inner, 0)
            for copy in sends:
                copy.wait_recv()
            for x, here, there in ((0, slab > 0, 0), (nx - 1, slab < n_slab - 1, 1)):
                gain = jnp.where(here, 0.12, 0.0)
                pots[step + 1, x] += gain * state[GATES + 1, x] * (
                    halo_x[step, there] - pots[step, x]
                )

            for x in range(nx):
                volts = pots[step, x]
                beyond = jnp.where(low_y, halo_y[step, 0, x : x + 1, :] - volts, 0.0)
                beyond += jnp.where(high_y, halo_y[step, 1, x : x + 1, :] - volts, 0.0)
                fresh = pots[step + 1, x] + 0.04 * state[GATES + 1, x] * beyond
                pots[step + 1, x] = fresh
                if step + 1 < STEPS:
                    faces[step + 1, 0, x : x + 1, :] = fresh[:1]
                    faces[step + 1, 1, x : x + 1, :] = fresh[ny - 1 :]
                else:
                    state[0, x] = fresh
            if step + 1 < STEPS:
                sends = place_.exchange(step + 1, pots.at[step + 1, 0], pots.at[step + 1, nx - 1], *links)
                for copy in sends:
                    copy.start()
                started += sends

        final = pots[STEPS].reshape(lines, nz)
        source = jnp.concatenate([final[:, :LANES], final[:, LANES:]], axis=0)
        rows = matmul(picks[...], split_halves(source), ((1,), (0,)))
        rows_out[:, :4, :] = rows.reshape(n_slab, 4, LANES)
        for copy in started:
            copy.wait_send()

    pl.when(place_.sec == 0)(heart)


def torso_kernel(
    n_slab, n_col,
    vol, state, rows_out, out,
    pots, coef, coef_src, faces, halo_x, halo_y, rows_in,
    load_sem, send_sem, recv_sem, row_sem,
):
    place_ = Place(n_slab, n_col, vol.shape)
    slab, col, sub, lane = place_.slab, place_.col, place_.sub, place_.lane
    low_y, high_y = place_.low_y, place_.high_y
    nx, ny, nz = vol.shape[2:]
    tx = SEGMENTS * nx
    barrier = pltpu.get_barrier_semaphore()

    def heart():
        keep = load(state, out.at[0], load_sem.at[0])
        pl.semaphore_wait(barrier, n_slab)

        def send(i, _):
            there = lax.rem(slab + i, n_slab)
            pltpu.make_async_remote_copy(
                src_ref=rows_out.at[there], dst_ref=rows_in.at[slab], send_sem=row_sem.at[0],
                recv_sem=row_sem.at[1], device_id=(1, there, col), device_id_type=MESH,
            ).start()
            return 0

        lax.fori_loop(0, n_slab, send, 0)
        keep.wait()
        wait_whole(rows_out, row_sem.at[0])

    def torso():
        def field(ref, f):
            return ref.at[0, pl.ds(SEGMENTS * f, SEGMENTS)]

        loads = [
            load(field(vol, 0), pots.at[0], load_sem.at[0]),
            load(field(vol, 2), field(out, 2), load_sem.at[1]),
            load(field(vol, 3), coef_src, load_sem.at[2]),
            load(field(vol, 1), field(out, 1), load_sem.at[3]),
        ]
        place_.greet()

        def invite(i, _):
            pl.semaphore_signal(
                barrier, inc=1, device_id=(0, lax.rem(slab + i, n_slab), col), device_id_type=MESH
            )
            return 0

        lax.fori_loop(0, n_slab, invite, 0)
        loads[0].wait()
        for face, row in enumerate((0, ny - 1)):
            for x in range(tx):
                faces[0, face, x : x + 1, :] = pots[0, x // nx, x % nx, row : row + 1, :]
        pl.semaphore_wait(barrier, 4)
        links = (faces, halo_x, halo_y, send_sem, recv_sem)
        sends = place_.exchange(0, pots.at[0, 0, 0], pots.at[0, SEGMENTS - 1, nx - 1], *links)
        for copy in sends:
            copy.start()
        for copy in loads[1:]:
            copy.wait()

        started = list(sends)
        mass = field(out, 2)
        for step in range(STEPS):
            now = pots.at[step]
            fresh_ref = pots.at[step + 1]
            before = pots.at[step - 1] if step else field(out, 1)

            def inner(k, _):
                planes = [now[k, r] for r in range(nx)]
                below = jnp.where(k > 0, now[jnp.maximum(k - 1, 0), nx - 1], 0.0)
                above = jnp.where(k < SEGMENTS - 1, now[jnp.minimum(k + 1, SEGMENTS - 1), 0], 0.0)
                around = [below] + planes + [above]
                for r in range(nx):
                    here = planes[r]
                    beside = around[r] + around[r + 2]
                    beside += jnp.where(sub == 0, 0.0, pltpu.roll(here, 1, 0))
                    beside += jnp.where(sub == ny - 1, 0.0, pltpu.roll(here, ny - 1, 0))
                    beside += jnp.where(lane == 0, 0.0, pltpu.roll(here, 1, 1))
                    beside += jnp.where(lane == nz - 1, 0.0, pltpu.roll(here, nz - 1, 1))
                    if step == 0:
                        gain = relax_omega / (6.0 + mass[k, r])
                        drive = gain * coef_src[k, r]
                        coef[k, r] = gain
                        coef_src[k, r] = drive
                    else:
                        gain = coef[k, r]
                        drive = coef_src[k, r]
                    fresh_ref[k, r] = (
                        drive + (1.0 - relax_omega) * before[k, r] + gain * beside
                    )
                return 0

            lax.fori_loop(0, SEGMENTS, inner, 0)
            for copy in sends:
                copy.wait_recv()
            for k, r, here, there in (
                (0, 0, slab > 0, 0), (SEGMENTS - 1, nx - 1, slab < n_slab - 1, 1),
            ):
                fresh_ref[k, r] += jnp.where(here, 1.0, 0.0) * coef[k, r] * halo_x[step, there]

            def outer(k, _):
                base = k * nx
                low = halo_y[step, 0, pl.ds(base, nx), :]
                high = halo_y[step, 1, pl.ds(base, nx), :]
                for r in range(nx):
                    beyond = jnp.where(low_y, low[r : r + 1], 0.0)
                    beyond += jnp.where(high_y, high[r : r + 1], 0.0)
                    fresh = fresh_ref[k, r] + coef[k, r] * beyond
                    fresh_ref[k, r] = fresh
                    if step + 1 < STEPS:
                        faces[step + 1, 0, pl.ds(base + r, 1), :] = fresh[:1]
                        faces[step + 1, 1, pl.ds(base + r, 1), :] = fresh[ny - 1 :]
                    if step + 2 == STEPS:
                        out[0, SEGMENTS + k, r] = fresh
                    if step + 1 == STEPS:
                        out[0, k, r] = fresh
                return 0

            lax.fori_loop(0, SEGMENTS, outer, 0)
            if step + 1 < STEPS:
                sends = place_.exchange(
                    step + 1, fresh_ref.at[0, 0], fresh_ref.at[SEGMENTS - 1, nx - 1], *links
                )
                for copy in sends:
                    copy.start()
                started += sends

        wait_whole(rows_in, row_sem.at[1])
        marks = jnp.where(
            iota((n_slab, LANES), 0) == iota((n_slab, LANES), 1) % n_slab, rows_in[:, 4, :], 0.0
        )
        marks = jnp.sum(marks, axis=0, keepdims=True)[:, : CAP * n_slab]
        goals = iota((tx * ny, CAP * n_slab), 0).astype(jnp.float32)
        hits = (goals == marks).astype(jnp.float32).astype(jnp.bfloat16)
        got = jnp.concatenate(
            [
                jnp.concatenate([rows_in[:, 2 * r + h, :] for r in range(CAP)], axis=0)
                for h in range(2)
            ],
            axis=1,
        )
        inflow = matmul(jnp.concatenate([hits, hits], axis=1), split_halves(got), ((1,), (0,)))
        out[0, pl.ds(3 * SEGMENTS, SEGMENTS)] = inflow.reshape(SEGMENTS, nx, ny, nz)
        for copy in started:
            copy.wait_send()

    pl.when(place_.sec == 0)(heart)
    pl.when(place_.sec == 1)(torso)


def solution(mesh):
    n_slab, n_col = mesh.shape["slab"], mesh.shape["col"]

    def on_device(volume, epi_line, epi_dest, epi_target):
        _, fields, nx, ny, nz = volume.shape
        epi = epi_line.shape[-1]
        tx = SEGMENTS * nx
        f32, dma = jnp.float32, pltpu.SemaphoreType.DMA
        fields_type = jax.ShapeDtypeStruct((fields, nx, ny, nz), f32)
        volume, epi_line, epi_dest, epi_target = (
            pltpu.with_memory_space_constraint(x, pltpu.HBM)
            for x in (volume, epi_line, epi_dest.reshape(epi_line.shape), epi_target)
        )
        hbm = pl.BlockSpec(memory_space=pltpu.HBM)
        vmem = pl.BlockSpec(memory_space=pltpu.VMEM)
        state, rows = pl.pallas_call(
            functools.partial(heart_kernel, n_slab, n_col),
            out_shape=(fields_type, jax.ShapeDtypeStruct((n_slab, 5, LANES), f32)),
            in_specs=[hbm] * 4,
            out_specs=(vmem, vmem),
            scratch_shapes=[
                pltpu.VMEM((STEPS + 1, nx, ny, nz), f32),
                pltpu.VMEM((STEPS, 2, nx, nz), f32),
                pltpu.VMEM((STEPS, 2, ny, nz), f32),
                pltpu.VMEM((STEPS, 2, nx, nz), f32),
                pltpu.VMEM((4 * n_slab, 4 * nx * ny), jnp.bfloat16),
                pltpu.VMEM((3, 1, epi), jnp.int32),
                dma((2,)), dma((3,)), dma((STEPS, 4)), dma((STEPS, 4)),
            ],
            compiler_params=pltpu.CompilerParams(
                collective_id=0, has_side_effects=True, vmem_limit_bytes=VMEM_LIMIT
            ),
        )(volume, epi_line, epi_dest, epi_target)
        return pl.pallas_call(
            functools.partial(torso_kernel, n_slab, n_col),
            out_shape=jax.ShapeDtypeStruct(volume.shape, f32),
            in_specs=[hbm, vmem, vmem],
            out_specs=vmem,
            scratch_shapes=[
                pltpu.VMEM((STEPS + 1, SEGMENTS, nx, ny, nz), f32),
                pltpu.VMEM((SEGMENTS, nx, ny, nz), f32),
                pltpu.VMEM((SEGMENTS, nx, ny, nz), f32),
                pltpu.VMEM((STEPS, 2, tx, nz), f32),
                pltpu.VMEM((STEPS, 2, ny, nz), f32),
                pltpu.VMEM((STEPS, 2, tx, nz), f32),
                pltpu.VMEM((n_slab, 5, LANES), f32),
                dma((4,)), dma((STEPS, 4)), dma((STEPS, 4)), dma((2,)),
            ],
            compiler_params=pltpu.CompilerParams(
                collective_id=1, has_side_effects=True, vmem_limit_bytes=VMEM_LIMIT
            ),
        )(volume, state, rows)

    return jax.shard_map(
        on_device,
        mesh=mesh,
        in_specs=(
            P("sec", None, "slab", "col", None),
            P("slab", "col", None),
            P("slab", "col", None, None),
            P("slab", "col", None),
        ),
        out_specs=P("sec", None, "slab", "col", None),
        check_vma=False,
    )
```

```python
import functools

import jax
import jax.numpy as jnp
import numpy as np
from jax import lax
from jax.experimental import pallas as pl
from jax.experimental.pallas import tpu as pltpu
from jax.sharding import PartitionSpec as P

STEPS = 4
CAP = 2
GATES = 18
LANES = 128
SEGMENTS = 5
WIDE = 2
PHASES = STEPS // WIDE
VMEM_LIMIT = 24 * 1024 * 1024
MESH = pl.DeviceIdType.MESH

gate_half = np.linspace(-1.5, 1.5, GATES)
gate_slope = 0.3 + 0.1 * (np.arange(GATES) % 4)
gate_decay = np.exp(-1.0 / (2.0 * 30.0 ** (np.arange(GATES) / 17.0)))
gate_conduct = 0.02 + 0.01 * (np.arange(GATES) % 3)
gate_reversal = np.linspace(-1.0, 1.0, GATES)
relax_omega = 1.5625


def iota(shape, dim):
    return lax.broadcasted_iota(jnp.int32, shape, dim)


def split_halves(x):
    high = x.astype(jnp.bfloat16)
    low = (x - high.astype(jnp.float32)).astype(jnp.bfloat16)
    return jnp.concatenate([high, low], axis=0)


def matmul(a, b, contract):
    return lax.dot_general(
        a, b, (contract, ((), ())), preferred_element_type=jnp.float32
    )


class Place:
    def __init__(self, n_slab, n_col, sizes):
        self.n_slab, self.n_col = n_slab, n_col
        self.sec = sec = lax.axis_index("sec")
        self.slab = slab = lax.axis_index("slab")
        self.col = col = lax.axis_index("col")
        _, _, nx, self.ny, self.nz = sizes
        plane = (self.ny, self.nz)
        self.sub, self.lane = iota(plane, 0), iota(plane, 1)
        self.exists = exists = ((slab > 0, slab < n_slab - 1), (col > 0, col < n_col - 1))
        self.low_y = jnp.logical_and(self.sub == 0, exists[1][0])
        self.high_y = jnp.logical_and(self.sub == self.ny - 1, exists[1][1])
        moves = [(i, j) for i in range(2) for j in range(2)]
        self.met = [
            (jnp.logical_and(exists[0][i], exists[1][j]), (sec, slab + 2 * i - 1, col + 2 * j - 1))
            for i, j in moves
        ]
        self.met += [(exists[0][i], (sec, slab + 2 * i - 1, col)) for i in range(2)]
        self.met += [(exists[1][j], (sec, slab, col + 2 * j - 1)) for j in range(2)]

    def greet(self):
        for here, there in self.met:

            @pl.when(here)
            def _(there=there):
                pl.semaphore_signal(
                    pltpu.get_barrier_semaphore(), inc=1, device_id=there, device_id_type=MESH
                )

    def await_met(self):
        count = sum(here.astype(jnp.int32) for here, _ in self.met)
        pl.semaphore_wait(pltpu.get_barrier_semaphore(), count)

    def exchange(self, phase, parts, send_sem, recv_sem):
        copies = []
        for way, (direction, src, dst) in parts:
            here, there = self.met[direction]
            copy = pltpu.make_async_remote_copy(
                src_ref=src, dst_ref=dst, send_sem=send_sem.at[phase, way],
                recv_sem=recv_sem.at[phase, way], device_id=there, device_id_type=MESH,
            )
            copies.append((here, copy, self.met[(3, 2, 1, 0, 5, 4, 7, 6)[direction]][0]))
        return copies

    def edges(self, phase, out_x, out_y, in_x, in_y, first, count):
        fields = pl.ds(first, count)
        return [
            (4 + 2 * axis + side, out.at[phase, side, fields], into.at[phase, 1 - side, fields])
            for axis, (out, into) in enumerate(((out_x, in_x), (out_y, in_y)))
            for side in range(2)
        ]

    def corners(self, phase, out_c, in_c):
        return [(c, out_c.at[phase, c], in_c.at[phase, 3 - c]) for c in range(4)]

    def beside_lines(self, cells, low, high):
        last = self.ny - 1
        below = jnp.where(self.sub == 0, low, pltpu.roll(cells, 1, 0))
        return below + jnp.where(self.sub == last, high, pltpu.roll(cells, last, 0))

    def beside_z(self, cells, low, high):
        last = self.nz - 1
        below = jnp.where(self.lane == 0, low, pltpu.roll(cells, 1, 1))
        return below + jnp.where(self.lane == last, high, pltpu.roll(cells, last, 1))


def start(copies):
    for here, copy, _ in copies:
        pl.when(here)(copy.start)


def wait_recv(copies):
    for _, copy, here in copies:
        pl.when(here)(copy.wait_recv)


def wait_send(copies):
    for here, copy, _ in copies:
        pl.when(here)(copy.wait_send)


def load(src, dst, sem):
    copy = pltpu.make_async_copy(src, dst, sem)
    copy.start()
    return copy


def wait_whole(ref, sem):
    pltpu.make_async_copy(ref, ref, sem).wait()


def heart_kernel(
    n_slab, n_col,
    vol, line_hbm, dest_hbm, target_hbm, state, rows_out,
    pots, moments, out_x, out_y, out_c, in_x, in_y, in_c, ring, picks, meta,
    load_sem, meta_sem, send_sem, recv_sem,
):
    place_ = Place(n_slab, n_col, vol.shape)
    low_y, high_y = place_.low_y, place_.high_y
    nx, ny, nz = vol.shape[2:]
    ends_x, ends_y = (0, nx - 1), (0, ny - 1)

    def bends(volts):
        scaled = {}
        for j in range(GATES):
            slope = float(0.5 / gate_slope[j])
            if slope not in scaled:
                scaled[slope] = volts * slope
            yield j, jnp.tanh(scaled[slope] - float(gate_half[j] * slope))

    def step_plane(step, x, with_moments):
        volts = pots[step, x]
        sigma = state[GATES + 1, x]
        beside_x = pots[step, jnp.maximum(x - 1, 0)] + pots[step, jnp.minimum(x + 1, nx - 1)]
        around = place_.beside_lines(volts, volts, volts)
        around += place_.beside_z(volts, volts, volts)
        flux = 0.12 * (beside_x - 2.0 * volts) + 0.04 * (around - 4.0 * volts)
        sums, weighted = {}, {}
        later, later_weighted = 0.0, 0.0
        for j, bend in bends(volts):
            rest = float(0.5 * (1.0 - gate_decay[j]))
            gate = state[1 + j, x] * float(gate_decay[j]) + (rest * bend + rest)
            state[1 + j, x] = gate
            conduct = float(gate_conduct[j])
            drawn = gate * float(gate_reversal[j])
            if conduct in sums:
                sums[conduct] += gate
                weighted[conduct] += drawn
            else:
                sums[conduct], weighted[conduct] = gate, drawn
            if with_moments:
                later += gate * float(gate_conduct[j] * gate_decay[j])
                later_weighted += drawn * float(gate_conduct[j] * gate_decay[j])
        if with_moments:
            moments[0, x] = later
            moments[1, x] = later_weighted
        current = sum(c * (volts * sums[c] - weighted[c]) for c in sums)
        pots[step + 1, x] = volts + sigma * flux - current

    def first_moments(x, _):
        later, later_weighted = 0.0, 0.0
        for j in range(GATES):
            part = state[1 + j, x] * float(gate_conduct[j] * gate_decay[j])
            later += part
            later_weighted += part * float(gate_reversal[j])
        moments[0, x] = later
        moments[1, x] = later_weighted
        return 0

    def send_edges(phase):
        step = WIDE * phase
        for side in range(2):
            out_x[phase, side, 0] = pots[step, ends_x[side]]
            for x in range(nx):
                y = ends_y[side]
                out_y[phase, side, 0, x : x + 1, :] = pots[step, x, y : y + 1, :]
        parts = place_.edges(phase, out_x, out_y, in_x, in_y, 0, 1)
        copies = place_.exchange(phase, list(enumerate(parts)), send_sem, recv_sem)
        start(copies)
        return copies

    def send_rest(phase):
        step = WIDE * phase
        for side in range(2):
            x = ends_x[side]
            out_x[phase, side, 1] = pots[step, x + 1 - 2 * side]
            out_x[phase, side, 2] = moments[0, x]
            out_x[phase, side, 3] = moments[1, x]
            if phase == 0:
                out_x[phase, side, 4] = state[GATES + 1, x]
            for j, y in enumerate(ends_y):
                out_c[phase, 2 * side + j] = pots[step, x, y : y + 1, :]
        for x in range(nx):
            for side, y in enumerate(ends_y):
                inward = y + 1 - 2 * side
                rows = [pots[step, x, inward : inward + 1, :]]
                rows += [moments[f, x, y : y + 1, :] for f in range(2)]
                if phase == 0:
                    rows.append(state[GATES + 1, x, y : y + 1, :])
                for f, row in enumerate(rows):
                    out_y[phase, side, 1 + f, x : x + 1, :] = row
        parts = place_.edges(phase, out_x, out_y, in_x, in_y, 1, 4 if phase == 0 else 3)
        parts += place_.corners(phase, out_c, in_c)
        copies = place_.exchange(phase, list(enumerate(parts, 4)), send_sem, recv_sem)
        start(copies)
        return copies

    def correct(step, planes, rows):
        for side, x in enumerate(ends_x):
            beyond = jnp.where(place_.exists[0][side], planes[side][...] - pots[step, x], 0.0)
            pots[step + 1, x] += 0.12 * state[GATES + 1, x] * beyond
        for x in range(nx):
            volts = pots[step, x]
            beyond = jnp.where(low_y, rows[0][x : x + 1, :] - volts, 0.0)
            beyond += jnp.where(high_y, rows[1][x : x + 1, :] - volts, 0.0)
            pots[step + 1, x] += 0.04 * state[GATES + 1, x] * beyond

    def step_ring(phase):
        step = WIDE * phase
        for axis, (into, across, along) in enumerate(((in_x, 0.12, 0.04), (in_y, 0.04, 0.12))):
            for side in range(2):
                volts, far = into[phase, side, 0], into[phase, side, 1]
                near = pots[step, ends_x[side]] if axis == 0 else out_y[phase, side, 0]
                tips = []
                for end in range(2):
                    corner = in_c[phase, 2 * side + end if axis == 0 else 2 * end + side]
                    own = volts[ends_y[end] : ends_y[end] + 1]
                    tips.append(jnp.where(place_.exists[1 - axis][end], corner, own))
                flux = across * (near + far - 2.0 * volts)
                flux += along * (place_.beside_lines(volts, *tips) - 2.0 * volts)
                flux += 0.04 * (place_.beside_z(volts, volts, volts) - 2.0 * volts)
                gain = np.float64(0.5) * gate_conduct * (1.0 - gate_decay)
                drawn, weighted = 0.0, 0.0
                for j, bend in bends(volts):
                    drawn += bend * float(gain[j])
                    weighted += bend * float(gain[j] * gate_reversal[j])
                drawn += into[phase, side, 2] + float(gain.sum())
                weighted += into[phase, side, 3] + float((gain * gate_reversal).sum())
                fresh = volts + in_sigma(axis, side) * flux - (volts * drawn - weighted)
                ring[phase, 2 * axis + side] = fresh

    def in_sigma(axis, side):
        return (in_x, in_y)[axis][0, side, 4]

    def heart():
        loads = [
            load(vol.at[0, 0], pots.at[0], load_sem.at[0]),
            load(vol.at[0, pl.ds(1, GATES + 1)], state.at[pl.ds(1, GATES + 1)], load_sem.at[1]),
        ]
        metas = [
            load(src.at[0], meta.at[i], meta_sem.at[i])
            for i, src in enumerate((line_hbm, dest_hbm, target_hbm))
        ]
        place_.greet()
        loads[0].wait()
        place_.await_met()
        edges = send_edges(0)
        loads[1].wait()
        lax.fori_loop(0, nx, first_moments, 0, unroll=2)
        rest = send_rest(0)
        started = edges + rest

        for copy in metas:
            copy.wait()
        lines = nx * ny
        fill_picks(lines)
        for phase in range(PHASES):
            step = WIDE * phase

            def first(x, _):
                step_plane(step, x, False)
                return 0

            def second(x, _):
                step_plane(step + 1, x, phase + 1 < PHASES)
                return 0

            lax.fori_loop(0, nx, first, 0, unroll=2)
            wait_recv(edges)
            correct(
                step, [in_x.at[phase, side, 0] for side in range(2)],
                [in_y.at[phase, side, 0] for side in range(2)],
            )
            lax.fori_loop(0, nx, second, 0, unroll=2)
            wait_recv(rest)
            step_ring(phase)
            correct(
                step + 1, [ring.at[phase, side] for side in range(2)],
                [ring.at[phase, 2 + side] for side in range(2)],
            )
            if phase + 1 < PHASES:
                edges = send_edges(phase + 1)
                rest = send_rest(phase + 1)
                started += edges + rest

        state[0] = pots[STEPS]
        final = pots[STEPS].reshape(lines, nz)
        source = jnp.concatenate([final[:, :LANES], final[:, LANES:]], axis=0)
        rows = matmul(picks[...], split_halves(source), ((1,), (0,)))
        rows_out[:, :4, :] = rows.reshape(n_slab, 4, LANES)
        wait_send(started)

    def fill_picks(lines):
        epi = meta.shape[2]
        line, dest, target = meta[0], meta[1], meta[2]
        slots = 4 * n_slab
        own = iota((slots, epi), 0)
        marks = own // 4 == dest
        before = (iota((epi, epi), 0) < iota((epi, epi), 1)).astype(jnp.bfloat16)
        rank = matmul(marks.astype(jnp.float32).astype(jnp.bfloat16), before, ((1,), (0,)))
        wanted = ((own // 2) % 2).astype(jnp.float32)
        place = jnp.logical_and(marks, rank == wanted)
        half = (own % 2).astype(jnp.float32)
        place = place.astype(jnp.float32)
        places = jnp.concatenate([place * (1.0 - half), place * half], axis=1)
        held = (iota((lines, epi), 0) == line).astype(jnp.float32).astype(jnp.bfloat16)
        for h in range(2):
            part = matmul(
                places[:, h * epi : (h + 1) * epi].astype(jnp.bfloat16), held, ((1,), (1,))
            ).astype(jnp.bfloat16)
            picks[:, h * lines : (h + 1) * lines] = part
            picks[:, (h + 2) * lines : (h + 3) * lines] = part
        own_d = iota((n_slab, epi), 0)
        marks_d = own_d == dest
        rank_d = matmul(marks_d.astype(jnp.float32).astype(jnp.bfloat16), before, ((1,), (0,)))
        goals = []
        for r in range(CAP):
            chosen = jnp.logical_and(marks_d, rank_d == float(r))
            goal = jnp.where(chosen, (target + 1).astype(jnp.float32), 0.0)
            goals.append(jnp.sum(goal, axis=1, keepdims=True) - 1.0)
        lane_s = iota((n_slab, LANES), 1)
        rows_out[:, 4, :] = jnp.where(lane_s < n_slab, goals[0], goals[1])

    pl.when(place_.sec == 0)(heart)


def torso_kernel(
    n_slab, n_col,
    vol, rows_out, out, rows_in,
    pots, coef, drive, out_x, out_y, out_c, in_x, in_y, in_c, ring_x, ring_y,
    load_sem, send_sem, recv_sem, row_sem,
):
    place_ = Place(n_slab, n_col, vol.shape)
    slab, col = place_.slab, place_.col
    low_y, high_y = place_.low_y, place_.high_y
    nx, ny, nz = vol.shape[2:]
    tx = SEGMENTS * nx
    barrier = pltpu.get_barrier_semaphore()
    ends = ((0, 0), (SEGMENTS - 1, nx - 1))
    before_last = 1.0 - relax_omega

    def field(f):
        return vol.at[0, pl.ds(SEGMENTS * f, SEGMENTS)]

    def before(step):
        return pots.at[step - 1] if step else out.at[1]

    def coefficients(k, _):
        for r in range(nx):
            gain = relax_omega / (6.0 + out[2, k, r])
            coef[k, r] = gain
            drive[k, r] = gain * drive[k, r]
        return 0

    def send_edges(phase):
        step = WIDE * phase
        for side, (k, r) in enumerate(ends):
            out_x[phase, side, 0] = pots[step, k, r]

        def pack(k, _):
            for r in range(nx):
                for side, y in enumerate((0, ny - 1)):
                    row = pots[step, k, r, y : y + 1, :]
                    out_y[phase, side, 0, pl.ds(k * nx + r, 1), :] = row
            return 0

        lax.fori_loop(0, SEGMENTS, pack, 0)
        parts = place_.edges(phase, out_x, out_y, in_x, in_y, 0, 1)
        copies = place_.exchange(phase, list(enumerate(parts)), send_sem, recv_sem)
        start(copies)
        return copies

    def send_rest(phase):
        step = WIDE * phase
        old = before(step)
        for side, (k, r) in enumerate(ends):
            out_x[phase, side, 1] = pots[step, k, r + 1 - 2 * side]
            out_x[phase, side, 2] = before_last * old[k, r] + drive[k, r]
            if phase == 0:
                out_x[phase, side, 3] = coef[k, r]
            for j, y in enumerate((0, ny - 1)):
                out_c[phase, 2 * side + j] = pots[step, k, r, y : y + 1, :]

        def pack(k, _):
            for r in range(nx):
                added = before_last * old[k, r] + drive[k, r]
                for side, y in enumerate((0, ny - 1)):
                    inward = y + 1 - 2 * side
                    rows = [pots[step, k, r, inward : inward + 1, :], added[y : y + 1]]
                    if phase == 0:
                        rows.append(coef[k, r, y : y + 1, :])
                    for f, row in enumerate(rows):
                        out_y[phase, side, 1 + f, pl.ds(k * nx + r, 1), :] = row
            return 0

        lax.fori_loop(0, SEGMENTS, pack, 0)
        parts = place_.edges(phase, out_x, out_y, in_x, in_y, 1, 3 if phase == 0 else 2)
        parts += place_.corners(phase, out_c, in_c)
        copies = place_.exchange(phase, list(enumerate(parts, 4)), send_sem, recv_sem)
        start(copies)
        return copies

    def sweep(step):
        old = before(step)

        def segment(k, _):
            planes = [pots[step, k, r] for r in range(nx)]
            below = jnp.where(k > 0, pots[step, jnp.maximum(k - 1, 0), nx - 1], 0.0)
            above = jnp.where(
                k < SEGMENTS - 1, pots[step, jnp.minimum(k + 1, SEGMENTS - 1), 0], 0.0
            )
            around = [below] + planes + [above]
            for r in range(nx):
                beside = around[r] + around[r + 2]
                beside += place_.beside_lines(planes[r], 0.0, 0.0)
                beside += place_.beside_z(planes[r], 0.0, 0.0)
                pots[step + 1, k, r] = drive[k, r] + before_last * old[k, r] + coef[k, r] * beside
            return 0

        lax.fori_loop(0, SEGMENTS, segment, 0)

    def correct(step, planes, rows):
        for side, (k, r) in enumerate(ends):
            beyond = jnp.where(place_.exists[0][side], planes[side][...], 0.0)
            pots[step + 1, k, r] += coef[k, r] * beyond

        def segment(k, _):
            low, high = (face[pl.ds(k * nx, nx), :] for face in rows)
            for r in range(nx):
                beyond = jnp.where(low_y, low[r : r + 1], 0.0)
                beyond += jnp.where(high_y, high[r : r + 1], 0.0)
                fresh = pots[step + 1, k, r] + coef[k, r] * beyond
                pots[step + 1, k, r] = fresh
                if step + 2 == STEPS:
                    out[1, k, r] = fresh
                if step + 1 == STEPS:
                    out[0, k, r] = fresh
            return 0

        lax.fori_loop(0, SEGMENTS, segment, 0)

    def step_ring(phase):
        step = WIDE * phase
        for side in range(2):
            cells = in_x[phase, side, 0]
            tips = [
                jnp.where(place_.exists[1][end], in_c[phase, 2 * side + end], 0.0)
                for end in range(2)
            ]
            beside = pots[step, *ends[side]] + in_x[phase, side, 1]
            beside += place_.beside_lines(cells, *tips) + place_.beside_z(cells, 0.0, 0.0)
            ring_x[phase, side] = in_x[phase, side, 2] + in_x[0, side, 3] * beside
        for side in range(2):
            tips = [
                jnp.where(place_.exists[0][end], in_c[phase, 2 * end + side], 0.0)
                for end in range(2)
            ]
            for k in range(SEGMENTS):
                rows = pl.ds(k * nx, nx)
                cells = in_y[phase, side, 0, rows, :]
                low = in_y[phase, side, 0, k * nx - 1 : k * nx, :] if k else tips[0]
                high = tips[1]
                if k + 1 < SEGMENTS:
                    high = in_y[phase, side, 0, (k + 1) * nx : (k + 1) * nx + 1, :]
                beside = out_y[phase, side, 0, rows, :] + in_y[phase, side, 1, rows, :]
                beside += place_.beside_lines(cells, low, high) + place_.beside_z(cells, 0.0, 0.0)
                ring_y[phase, side, rows, :] = (
                    in_y[phase, side, 2, rows, :] + in_y[0, side, 3, rows, :] * beside
                )

    def heart():
        pl.semaphore_wait(barrier, n_slab)
        n_ring = 4
        ring_size = n_slab // n_ring

        def send(i, _):
            there = ring_size * lax.rem(slab // ring_size + i, n_ring) + i // n_ring
            pltpu.make_async_remote_copy(
                src_ref=rows_out.at[there], dst_ref=rows_in.at[slab], send_sem=row_sem.at[0],
                recv_sem=row_sem.at[1], device_id=(1, there, col), device_id_type=MESH,
            ).start()
            return 0

        lax.fori_loop(0, n_slab, send, 0)
        wait_whole(rows_out, row_sem.at[0])

    def torso():
        loads = [
            load(field(0), pots.at[0], load_sem.at[0]),
            load(field(2), out.at[2], load_sem.at[1]),
            load(field(3), drive, load_sem.at[2]),
            load(field(1), out.at[1], load_sem.at[3]),
        ]
        place_.greet()

        def invite(i, _):
            there = (0, lax.rem(slab + i, n_slab), col)
            pl.semaphore_signal(barrier, inc=1, device_id=there, device_id_type=MESH)
            return 0

        lax.fori_loop(0, n_slab, invite, 0)
        loads[0].wait()
        place_.await_met()
        edges = send_edges(0)
        for copy in loads[1:]:
            copy.wait()
        lax.fori_loop(0, SEGMENTS, coefficients, 0)
        rest = send_rest(0)
        started = edges + rest
        for phase in range(PHASES):
            step = WIDE * phase
            sweep(step)
            wait_recv(edges)
            correct(
                step, [in_x.at[phase, side, 0] for side in range(2)],
                [in_y.at[phase, side, 0] for side in range(2)],
            )
            sweep(step + 1)
            wait_recv(rest)
            step_ring(phase)
            correct(
                step + 1, [ring_x.at[phase, side] for side in range(2)],
                [ring_y.at[phase, side] for side in range(2)],
            )
            if phase + 1 < PHASES:
                edges = send_edges(phase + 1)
                rest = send_rest(phase + 1)
                started += edges + rest

        wait_whole(rows_in, row_sem.at[1])
        wait_send(started)

    pl.when(place_.sec == 0)(heart)
    pl.when(place_.sec == 1)(torso)


def result_kernel(n_slab, state, fields, rows, out, inflow_ref, sems):
    nx, ny, nz = state.shape[1:]
    tx = SEGMENTS * nx
    sec = lax.axis_index("sec")

    def heart():
        load(state, out.at[0], sems.at[0]).wait()

    def torso():
        copies = [
            load(fields.at[f], out.at[0, pl.ds(SEGMENTS * f, SEGMENTS)], sems.at[f])
            for f in range(3)
        ]
        marks = jnp.where(
            iota((n_slab, LANES), 0) == iota((n_slab, LANES), 1) % n_slab, rows[:, 4, :], 0.0
        )
        marks = jnp.sum(marks, axis=0, keepdims=True)[:, : CAP * n_slab]
        goals = iota((tx * ny, CAP * n_slab), 0).astype(jnp.float32)
        hits = (goals == marks).astype(jnp.float32).astype(jnp.bfloat16)
        got = jnp.concatenate(
            [
                jnp.concatenate([rows[:, 2 * r + h, :] for r in range(CAP)], axis=0)
                for h in range(2)
            ],
            axis=1,
        )
        inflow = matmul(jnp.concatenate([hits, hits], axis=1), split_halves(got), ((1,), (0,)))
        inflow_ref[...] = inflow.reshape(SEGMENTS, nx, ny, nz)
        copies.append(load(inflow_ref, out.at[0, pl.ds(3 * SEGMENTS, SEGMENTS)], sems.at[3]))
        for copy in copies:
            copy.wait()

    pl.when(sec == 0)(heart)
    pl.when(sec == 1)(torso)


def solution(mesh):
    n_slab, n_col = mesh.shape["slab"], mesh.shape["col"]

    def on_device(volume, epi_line, epi_dest, epi_target):
        _, fields, nx, ny, nz = volume.shape
        epi = epi_line.shape[-1]
        tx = SEGMENTS * nx
        f32, dma = jnp.float32, pltpu.SemaphoreType.DMA
        fields_type = jax.ShapeDtypeStruct((fields, nx, ny, nz), f32)
        volume, epi_line, epi_dest, epi_target = (
            pltpu.with_memory_space_constraint(x, pltpu.HBM)
            for x in (volume, epi_line, epi_dest.reshape(epi_line.shape), epi_target)
        )
        hbm = pl.BlockSpec(memory_space=pltpu.HBM)
        vmem = pl.BlockSpec(memory_space=pltpu.VMEM)
        state, rows = pl.pallas_call(
            functools.partial(heart_kernel, n_slab, n_col),
            out_shape=(fields_type, jax.ShapeDtypeStruct((n_slab, 5, LANES), f32)),
            in_specs=[hbm] * 4,
            out_specs=(vmem, vmem),
            scratch_shapes=[
                pltpu.VMEM((STEPS + 1, nx, ny, nz), f32),
                pltpu.VMEM((2, nx, ny, nz), f32),
                pltpu.VMEM((PHASES, 2, 5, ny, nz), f32),
                pltpu.VMEM((PHASES, 2, 5, nx, nz), f32),
                pltpu.VMEM((PHASES, 4, 1, nz), f32),
                pltpu.VMEM((PHASES, 2, 5, ny, nz), f32),
                pltpu.VMEM((PHASES, 2, 5, nx, nz), f32),
                pltpu.VMEM((PHASES, 4, 1, nz), f32),
                pltpu.VMEM((PHASES, 4, ny, nz), f32),
                pltpu.VMEM((4 * n_slab, 4 * nx * ny), jnp.bfloat16),
                pltpu.VMEM((3, 1, epi), jnp.int32),
                dma((2,)), dma((3,)), dma((PHASES, 12)), dma((PHASES, 12)),
            ],
            compiler_params=pltpu.CompilerParams(
                collective_id=0, has_side_effects=True, vmem_limit_bytes=VMEM_LIMIT
            ),
        )(volume, epi_line, epi_dest, epi_target)
        fields, got = pl.pallas_call(
            functools.partial(torso_kernel, n_slab, n_col),
            out_shape=(
                jax.ShapeDtypeStruct((3, SEGMENTS, nx, ny, nz), f32),
                jax.ShapeDtypeStruct((n_slab, 5, LANES), f32),
            ),
            in_specs=[hbm, vmem],
            out_specs=(vmem, vmem),
            scratch_shapes=[
                pltpu.VMEM((STEPS + 1, SEGMENTS, nx, ny, nz), f32),
                pltpu.VMEM((SEGMENTS, nx, ny, nz), f32),
                pltpu.VMEM((SEGMENTS, nx, ny, nz), f32),
                pltpu.VMEM((PHASES, 2, 4, ny, nz), f32),
                pltpu.VMEM((PHASES, 2, 4, tx, nz), f32),
                pltpu.VMEM((PHASES, 4, 1, nz), f32),
                pltpu.VMEM((PHASES, 2, 4, ny, nz), f32),
                pltpu.VMEM((PHASES, 2, 4, tx, nz), f32),
                pltpu.VMEM((PHASES, 4, 1, nz), f32),
                pltpu.VMEM((PHASES, 2, ny, nz), f32),
                pltpu.VMEM((PHASES, 2, tx, nz), f32),
                dma((4,)), dma((PHASES, 12)), dma((PHASES, 12)), dma((2,)),
            ],
            compiler_params=pltpu.CompilerParams(
                collective_id=1, has_side_effects=True, vmem_limit_bytes=VMEM_LIMIT
            ),
        )(volume, rows)
        return pl.pallas_call(
            functools.partial(result_kernel, n_slab),
            out_shape=jax.ShapeDtypeStruct(volume.shape, f32),
            in_specs=[vmem, vmem, vmem],
            out_specs=hbm,
            scratch_shapes=[pltpu.VMEM((SEGMENTS, nx, ny, nz), f32), dma((4,))],
            compiler_params=pltpu.CompilerParams(vmem_limit_bytes=VMEM_LIMIT),
        )(state, fields, got)

    return jax.shard_map(
        on_device,
        mesh=mesh,
        in_specs=(
            P("sec", None, "slab", "col", None),
            P("slab", "col", None),
            P("slab", "col", None, None),
            P("slab", "col", None),
        ),
        out_specs=P("sec", None, "slab", "col", None),
        check_vma=False,
    )
```

```python
import functools

import jax
import jax.numpy as jnp
import numpy as np
from jax import lax
from jax.experimental import pallas as pl
from jax.experimental.pallas import tpu as pltpu
from jax.sharding import PartitionSpec as P

STEPS = 4
CAP = 2
GATES = 18
LANES = 128
NARROW = 8
SEGMENTS = 5
N_RING = 4
WIDE = 2
PHASES = STEPS // WIDE
VMEM_LIMIT = 24 * 1024 * 1024
MESH = pl.DeviceIdType.MESH

gate_half = np.linspace(-1.5, 1.5, GATES)
gate_slope = 0.3 + 0.1 * (np.arange(GATES) % 4)
gate_decay = np.exp(-1.0 / (2.0 * 30.0 ** (np.arange(GATES) / 17.0)))
gate_conduct = 0.02 + 0.01 * (np.arange(GATES) % 3)
gate_reversal = np.linspace(-1.0, 1.0, GATES)
relax_omega = 1.5625


def iota(shape, dim):
    return lax.broadcasted_iota(jnp.int32, shape, dim)


def split_halves(x):
    high = x.astype(jnp.bfloat16)
    low = (x - high.astype(jnp.float32)).astype(jnp.bfloat16)
    return jnp.concatenate([high, low], axis=0)


def matmul(a, b, contract):
    return lax.dot_general(
        a, b, (contract, ((), ())), preferred_element_type=jnp.float32
    )


class Place:
    def __init__(self, n_slab, n_col, sizes):
        self.n_slab, self.n_col = n_slab, n_col
        self.ring_size = n_slab // N_RING
        self.sec = sec = lax.axis_index("sec")
        self.slab = slab = lax.axis_index("slab")
        self.col = col = lax.axis_index("col")
        _, _, nx, self.ny, self.nz = sizes
        plane = (self.ny, self.nz)
        self.sub, self.lane = iota(plane, 0), iota(plane, 1)
        self.exists = exists = ((slab > 0, slab < n_slab - 1), (col > 0, col < n_col - 1))
        self.low_y = jnp.logical_and(self.sub == 0, exists[1][0])
        self.high_y = jnp.logical_and(self.sub == self.ny - 1, exists[1][1])
        moves = [(i, j) for i in range(2) for j in range(2)]
        self.met = [
            (jnp.logical_and(exists[0][i], exists[1][j]), (sec, slab + 2 * i - 1, col + 2 * j - 1))
            for i, j in moves
        ]
        self.met += [(exists[0][i], (sec, slab + 2 * i - 1, col)) for i in range(2)]
        self.met += [(exists[1][j], (sec, slab, col + 2 * j - 1)) for j in range(2)]

    def across(self, sec):
        return [
            (self.slab >= 0, (sec, lax.rem(self.slab + i * self.ring_size, self.n_slab), self.col))
            for i in range(N_RING)
        ]

    def greet(self, others):
        for here, there in self.met[4:] + others + self.met[:4]:

            @pl.when(here)
            def _(there=there):
                pl.semaphore_signal(
                    pltpu.get_barrier_semaphore(), inc=1, device_id=there, device_id_type=MESH
                )

    def await_met(self, others=()):
        count = sum(here.astype(jnp.int32) for here, _ in [*self.met, *others])
        pl.semaphore_wait(pltpu.get_barrier_semaphore(), count)

    def exchange(self, phase, parts, send_sem, recv_sem):
        copies = []
        for way, (direction, src, dst) in parts:
            here, there = self.met[direction]
            copy = pltpu.make_async_remote_copy(
                src_ref=src, dst_ref=dst, send_sem=send_sem.at[way],
                recv_sem=recv_sem.at[phase, way], device_id=there, device_id_type=MESH,
            )
            copies.append((here, copy, self.met[(3, 2, 1, 0, 5, 4, 7, 6)[direction]][0]))
        return copies

    def edges(self, phase, out_x, out_y, in_x, in_y, first, count):
        fields = pl.ds(first, count)
        return [
            (4 + 2 * axis + side, out.at[phase, side, fields], into.at[phase, 1 - side, fields])
            for axis, (out, into) in enumerate(((out_x, in_x), (out_y, in_y)))
            for side in range(2)
        ]

    def corners(self, phase, out_c, in_c):
        return [(c, out_c.at[phase, c], in_c.at[phase, 3 - c]) for c in range(4)]

    def beside_lines(self, cells, low, high):
        last = self.ny - 1
        below = jnp.where(self.sub == 0, low, pltpu.roll(cells, 1, 0))
        return below + jnp.where(self.sub == last, high, pltpu.roll(cells, last, 0))

    def beside_z(self, cells, low, high):
        last = self.nz - 1
        below = jnp.where(self.lane == 0, low, pltpu.roll(cells, 1, 1))
        return below + jnp.where(self.lane == last, high, pltpu.roll(cells, last, 1))


def start(copies):
    for here, copy, _ in copies:
        pl.when(here)(copy.start)


def wait_recv(copies):
    for _, copy, here in copies:
        pl.when(here)(copy.wait_recv)


def wait_send(copies):
    for here, copy, _ in copies:
        pl.when(here)(copy.wait_send)


def load(src, dst, sem):
    copy = pltpu.make_async_copy(src, dst, sem)
    copy.start()
    return copy


def wait_whole(ref, sem):
    pltpu.make_async_copy(ref, ref, sem).wait()


def heart_part(
    place_, vol, line_hbm, dest_hbm, target_hbm, state, rows_in, lines_in,
    pots, moments, out_x, out_y, out_c, in_x, in_y, in_c, ring, picks, meta, rows_out, lines_out,
    meta_sem, send_sem, recv_sem, row_sem, ready_sem,
):
    n_slab, slab, col = place_.n_slab, place_.slab, place_.col
    low_y, high_y = place_.low_y, place_.high_y
    nx, ny, nz = vol.shape[2:]
    ends_x, ends_y = (0, nx - 1), (0, ny - 1)

    def bends(volts):
        scaled = {}
        for j in range(GATES):
            slope = float(0.5 / gate_slope[j])
            if slope not in scaled:
                scaled[slope] = volts * slope
            yield j, jnp.tanh(scaled[slope] - float(gate_half[j] * slope))

    def step_plane(step, x, with_moments):
        volts = pots[step, x]
        sigma = state[GATES + 1, x]
        beside_x = pots[step, jnp.maximum(x - 1, 0)] + pots[step, jnp.minimum(x + 1, nx - 1)]
        around = place_.beside_lines(volts, volts, volts)
        around += place_.beside_z(volts, volts, volts)
        flux = 0.12 * (beside_x - 2.0 * volts) + 0.04 * (around - 4.0 * volts)
        sums, weighted = {}, {}
        later, later_weighted = 0.0, 0.0
        for j, bend in bends(volts):
            rest = float(0.5 * (1.0 - gate_decay[j]))
            gate = state[1 + j, x] * float(gate_decay[j]) + (rest * bend + rest)
            state[1 + j, x] = gate
            conduct = float(gate_conduct[j])
            drawn = gate * float(gate_reversal[j])
            if conduct in sums:
                sums[conduct] += gate
                weighted[conduct] += drawn
            else:
                sums[conduct], weighted[conduct] = gate, drawn
            if with_moments:
                later += gate * float(gate_conduct[j] * gate_decay[j])
                later_weighted += drawn * float(gate_conduct[j] * gate_decay[j])
        if with_moments:
            moments[0, x] = later
            moments[1, x] = later_weighted
        current = sum(c * (volts * sums[c] - weighted[c]) for c in sums)
        pots[step + 1, x] = volts + sigma * flux - current

    def first_moments(x, _):
        later, later_weighted = 0.0, 0.0
        for j in range(GATES):
            part = state[1 + j, x] * float(gate_conduct[j] * gate_decay[j])
            later += part
            later_weighted += part * float(gate_reversal[j])
        moments[0, x] = later
        moments[1, x] = later_weighted
        return 0

    def send_edges(phase):
        step = WIDE * phase
        for side in range(2):
            out_x[phase, side, 0] = pots[step, ends_x[side]]
            for x in range(nx):
                y = ends_y[side]
                out_y[phase, side, 0, x : x + 1, :] = pots[step, x, y : y + 1, :]
        parts = place_.edges(phase, out_x, out_y, in_x, in_y, 0, 1)
        copies = place_.exchange(phase, list(enumerate(parts)), send_sem, recv_sem)
        start(copies)
        return copies

    def send_rest(phase):
        step = WIDE * phase
        for side in range(2):
            x = ends_x[side]
            out_x[phase, side, 1] = pots[step, x + 1 - 2 * side]
            out_x[phase, side, 2] = moments[0, x]
            out_x[phase, side, 3] = moments[1, x]
            if phase == 0:
                out_x[phase, side, 4] = state[GATES + 1, x]
            for j, y in enumerate(ends_y):
                out_c[phase, 2 * side + j] = pots[step, x, y : y + 1, :]
        for x in range(nx):
            for side, y in enumerate(ends_y):
                inward = y + 1 - 2 * side
                rows = [pots[step, x, inward : inward + 1, :]]
                rows += [moments[f, x, y : y + 1, :] for f in range(2)]
                if phase == 0:
                    rows.append(state[GATES + 1, x, y : y + 1, :])
                for f, row in enumerate(rows):
                    out_y[phase, side, 1 + f, x : x + 1, :] = row
        parts = place_.edges(phase, out_x, out_y, in_x, in_y, 1, 4 if phase == 0 else 3)
        parts += place_.corners(phase, out_c, in_c)
        copies = place_.exchange(phase, list(enumerate(parts, 4)), send_sem, recv_sem)
        start(copies)
        return copies

    def correct(step, planes, rows):
        for side, x in enumerate(ends_x):
            beyond = jnp.where(place_.exists[0][side], planes[side][...] - pots[step, x], 0.0)
            pots[step + 1, x] += 0.12 * state[GATES + 1, x] * beyond
        for x in range(nx):
            volts = pots[step, x]
            beyond = jnp.where(low_y, rows[0][x : x + 1, :] - volts, 0.0)
            beyond += jnp.where(high_y, rows[1][x : x + 1, :] - volts, 0.0)
            pots[step + 1, x] += 0.04 * state[GATES + 1, x] * beyond

    def step_ring(phase):
        step = WIDE * phase
        for axis, (into, across, along) in enumerate(((in_x, 0.12, 0.04), (in_y, 0.04, 0.12))):
            for side in range(2):
                volts, far = into[phase, side, 0], into[phase, side, 1]
                near = pots[step, ends_x[side]] if axis == 0 else out_y[phase, side, 0]
                tips = []
                for end in range(2):
                    corner = in_c[phase, 2 * side + end if axis == 0 else 2 * end + side]
                    own = volts[ends_y[end] : ends_y[end] + 1]
                    tips.append(jnp.where(place_.exists[1 - axis][end], corner, own))
                flux = across * (near + far - 2.0 * volts)
                flux += along * (place_.beside_lines(volts, *tips) - 2.0 * volts)
                flux += 0.04 * (place_.beside_z(volts, volts, volts) - 2.0 * volts)
                gain = np.float64(0.5) * gate_conduct * (1.0 - gate_decay)
                drawn, weighted = 0.0, 0.0
                for j, bend in bends(volts):
                    drawn += bend * float(gain[j])
                    weighted += bend * float(gain[j] * gate_reversal[j])
                drawn += into[phase, side, 2] + float(gain.sum())
                weighted += into[phase, side, 3] + float((gain * gate_reversal).sum())
                fresh = volts + in_sigma(axis, side) * flux - (volts * drawn - weighted)
                ring[phase, 2 * axis + side] = fresh

    def in_sigma(axis, side):
        return (in_x, in_y)[axis][0, side, 4]

    def heart():
        loads = [
            load(vol.at[0, 0], pots.at[0], send_sem.at[4]),
            load(vol.at[0, pl.ds(1, GATES + 1)], state.at[pl.ds(1, GATES + 1)], send_sem.at[5]),
        ]
        metas = [
            load(src.at[0], meta.at[i], meta_sem.at[i])
            for i, src in enumerate((line_hbm, dest_hbm, target_hbm))
        ]
        place_.greet(place_.across(1))
        loads[0].wait()
        place_.await_met()
        edges = send_edges(0)
        loads[1].wait()
        lax.fori_loop(0, nx, first_moments, 0, unroll=2)
        rest = send_rest(0)

        for copy in metas:
            copy.wait()
        lines = nx * ny
        fill_picks(lines)
        for phase in range(PHASES):
            step = WIDE * phase

            def first(x, _):
                step_plane(step, x, False)
                return 0

            def second(x, _):
                step_plane(step + 1, x, phase + 1 < PHASES)
                return 0

            lax.fori_loop(0, nx, first, 0, unroll=2)
            wait_recv(edges)
            correct(
                step, [in_x.at[phase, side, 0] for side in range(2)],
                [in_y.at[phase, side, 0] for side in range(2)],
            )
            lax.fori_loop(0, nx, second, 0, unroll=2)
            wait_recv(rest)
            step_ring(phase)
            correct(
                step + 1, [ring.at[phase, side] for side in range(2)],
                [ring.at[phase, 2 + side] for side in range(2)],
            )
            if phase + 1 < PHASES:
                wait_send(edges + rest)
                edges = send_edges(phase + 1)
                rest = send_rest(phase + 1)

        state[0] = pots[STEPS]
        final = pots[STEPS].reshape(lines, nz)
        source = jnp.concatenate([final[:, :LANES], final[:, LANES:]], axis=0)
        rows = matmul(picks[...], split_halves(source), ((1,), (0,)))
        rows_out[...] = rows.reshape(n_slab, 4, LANES)
        pl.semaphore_wait(ready_sem, N_RING)

        def send(i, _):
            there = place_.ring_size * lax.rem(i, N_RING) + i // N_RING
            for f, (src, dst) in enumerate(((rows_out, rows_in), (lines_out, lines_in))):
                pltpu.make_async_remote_copy(
                    src_ref=src.at[there], dst_ref=dst.at[slab], send_sem=row_sem.at[f, 0],
                    recv_sem=row_sem.at[f, 1], device_id=(1, there, col), device_id_type=MESH,
                ).start()
            return 0

        lax.fori_loop(0, n_slab, send, 0)
        wait_whole(rows_out, row_sem.at[0, 0])
        wait_whole(lines_out, row_sem.at[1, 0])
        wait_send(edges + rest)

    def fill_picks(lines):
        epi = meta.shape[2]
        line, dest, target = meta[0], meta[1], meta[2]
        slots = 4 * n_slab
        own = iota((slots, epi), 0)
        marks = own // 4 == dest
        before = (iota((epi, epi), 0) < iota((epi, epi), 1)).astype(jnp.bfloat16)
        rank = matmul(marks.astype(jnp.float32).astype(jnp.bfloat16), before, ((1,), (0,)))
        wanted = ((own // 2) % 2).astype(jnp.float32)
        place = jnp.logical_and(marks, rank == wanted)
        half = (own % 2).astype(jnp.float32)
        place = place.astype(jnp.float32)
        places = jnp.concatenate([place * (1.0 - half), place * half], axis=1)
        held = (iota((lines, epi), 0) == line).astype(jnp.float32).astype(jnp.bfloat16)
        for h in range(2):
            part = matmul(
                places[:, h * epi : (h + 1) * epi].astype(jnp.bfloat16), held, ((1,), (1,))
            ).astype(jnp.bfloat16)
            picks[:, h * lines : (h + 1) * lines] = part
            picks[:, (h + 2) * lines : (h + 3) * lines] = part
        own_d = iota((n_slab, epi), 0)
        marks_d = own_d == dest
        rank_d = matmul(marks_d.astype(jnp.float32).astype(jnp.bfloat16), before, ((1,), (0,)))
        goals = []
        for r in range(CAP):
            chosen = jnp.logical_and(marks_d, rank_d == float(r))
            goal = jnp.where(chosen, (target + 1).astype(jnp.float32), 0.0)
            goals.append(jnp.sum(goal, axis=1, keepdims=True) - 1.0)
        lines_out[:, 0, :] = jnp.where(iota((n_slab, NARROW), 1) == 0, goals[0], goals[1])

    heart()


def torso_part(
    place_, vol, out, rows_in, lines_in,
    pots, coef, drive, out_x, out_y, out_c, in_x, in_y, in_c, ring_x, ring_y,
    send_sem, recv_sem, row_sem, ready_sem, round_sem,
):
    n_slab, slab, col = place_.n_slab, place_.slab, place_.col
    low_y, high_y = place_.low_y, place_.high_y
    nx, ny, nz = vol.shape[2:]
    tx = SEGMENTS * nx
    ends = ((0, 0), (SEGMENTS - 1, nx - 1))
    before_last = 1.0 - relax_omega

    def field(f):
        return vol.at[0, pl.ds(SEGMENTS * f, SEGMENTS)]

    def before(step):
        return pots.at[step - 1] if step else out.at[1]

    def coefficients(k, _):
        for r in range(nx):
            gain = relax_omega / (6.0 + out[2, k, r])
            coef[k, r] = gain
            drive[k, r] = gain * drive[k, r]
        return 0

    def send_edges(phase):
        step = WIDE * phase
        for side, (k, r) in enumerate(ends):
            out_x[phase, side, 0] = pots[step, k, r]

        def pack(k, _):
            for r in range(nx):
                for side, y in enumerate((0, ny - 1)):
                    row = pots[step, k, r, y : y + 1, :]
                    out_y[phase, side, 0, pl.ds(k * nx + r, 1), :] = row
            return 0

        lax.fori_loop(0, SEGMENTS, pack, 0)
        parts = place_.edges(phase, out_x, out_y, in_x, in_y, 0, 1)
        copies = place_.exchange(phase, list(enumerate(parts)), send_sem, recv_sem)
        start(copies)
        return copies

    def send_rest(phase):
        step = WIDE * phase
        old = before(step)
        for side, (k, r) in enumerate(ends):
            out_x[phase, side, 1] = pots[step, k, r + 1 - 2 * side]
            out_x[phase, side, 2] = before_last * old[k, r] + drive[k, r]
            if phase == 0:
                out_x[phase, side, 3] = coef[k, r]
            for j, y in enumerate((0, ny - 1)):
                out_c[phase, 2 * side + j] = pots[step, k, r, y : y + 1, :]

        def pack(k, _):
            for r in range(nx):
                added = before_last * old[k, r] + drive[k, r]
                for side, y in enumerate((0, ny - 1)):
                    inward = y + 1 - 2 * side
                    rows = [pots[step, k, r, inward : inward + 1, :], added[y : y + 1]]
                    if phase == 0:
                        rows.append(coef[k, r, y : y + 1, :])
                    for f, row in enumerate(rows):
                        out_y[phase, side, 1 + f, pl.ds(k * nx + r, 1), :] = row
            return 0

        lax.fori_loop(0, SEGMENTS, pack, 0)
        parts = place_.edges(phase, out_x, out_y, in_x, in_y, 1, 3 if phase == 0 else 2)
        parts += place_.corners(phase, out_c, in_c)
        copies = place_.exchange(phase, list(enumerate(parts, 4)), send_sem, recv_sem)
        start(copies)
        return copies

    def sweep(step):
        old = before(step)

        def segment(k, _):
            planes = [pots[step, k, r] for r in range(nx)]
            below = jnp.where(k > 0, pots[step, jnp.maximum(k - 1, 0), nx - 1], 0.0)
            above = jnp.where(
                k < SEGMENTS - 1, pots[step, jnp.minimum(k + 1, SEGMENTS - 1), 0], 0.0
            )
            around = [below] + planes + [above]
            for r in range(nx):
                beside = around[r] + around[r + 2]
                beside += place_.beside_lines(planes[r], 0.0, 0.0)
                beside += place_.beside_z(planes[r], 0.0, 0.0)
                pots[step + 1, k, r] = drive[k, r] + before_last * old[k, r] + coef[k, r] * beside
            return 0

        lax.fori_loop(0, SEGMENTS, segment, 0)

    def correct(step, planes, rows):
        for side, (k, r) in enumerate(ends):
            beyond = jnp.where(place_.exists[0][side], planes[side][...], 0.0)
            pots[step + 1, k, r] += coef[k, r] * beyond

        def segment(k, _):
            low, high = (face[pl.ds(k * nx, nx), :] for face in rows)
            for r in range(nx):
                beyond = jnp.where(low_y, low[r : r + 1], 0.0)
                beyond += jnp.where(high_y, high[r : r + 1], 0.0)
                fresh = pots[step + 1, k, r] + coef[k, r] * beyond
                pots[step + 1, k, r] = fresh
                if step + 2 == STEPS:
                    out[1, k, r] = fresh
                if step + 1 == STEPS:
                    out[0, k, r] = fresh
            return 0

        lax.fori_loop(0, SEGMENTS, segment, 0)

    def step_ring(phase):
        step = WIDE * phase
        for side in range(2):
            cells = in_x[phase, side, 0]
            tips = [
                jnp.where(place_.exists[1][end], in_c[phase, 2 * side + end], 0.0)
                for end in range(2)
            ]
            beside = pots[step, *ends[side]] + in_x[phase, side, 1]
            beside += place_.beside_lines(cells, *tips) + place_.beside_z(cells, 0.0, 0.0)
            ring_x[phase, side] = in_x[phase, side, 2] + in_x[0, side, 3] * beside
        for side in range(2):
            tips = [
                jnp.where(place_.exists[0][end], in_c[phase, 2 * end + side], 0.0)
                for end in range(2)
            ]
            for k in range(SEGMENTS):
                rows = pl.ds(k * nx, nx)
                cells = in_y[phase, side, 0, rows, :]
                low = in_y[phase, side, 0, k * nx - 1 : k * nx, :] if k else tips[0]
                high = tips[1]
                if k + 1 < SEGMENTS:
                    high = in_y[phase, side, 0, (k + 1) * nx : (k + 1) * nx + 1, :]
                beside = out_y[phase, side, 0, rows, :] + in_y[phase, side, 1, rows, :]
                beside += place_.beside_lines(cells, low, high) + place_.beside_z(cells, 0.0, 0.0)
                ring_y[phase, side, rows, :] = (
                    in_y[phase, side, 2, rows, :] + in_y[0, side, 3, rows, :] * beside
                )

    def torso():
        loads = [
            load(field(0), pots.at[0], send_sem.at[4]),
            load(field(2), out.at[2], send_sem.at[5]),
            load(field(3), drive, send_sem.at[6]),
            load(field(1), out.at[1], send_sem.at[7]),
        ]
        ring_size = place_.ring_size
        at = lax.rem(slab, ring_size)

        def along(k):
            return (1, slab - at + lax.rem(at + k + ring_size, ring_size), col)

        others = []
        reach = ring_size // 4
        if reach:
            others += [(at == 0, along(-1)), (at == ring_size - 1, along(1))]
        for k in range(2, reach + 1):
            others += [(slab >= 0, along(k)), (slab >= 0, along(-k))]
        place_.greet(others)

        hearts = place_.across(0)
        place_.await_met(others + hearts)
        if reach:
            for k in (reach, -reach):
                pl.semaphore_signal(round_sem, inc=1, device_id=along(k), device_id_type=MESH)
        loads[0].wait()
        edges = send_edges(0)
        for copy in loads[1:]:
            copy.wait()
        lax.fori_loop(0, SEGMENTS, coefficients, 0)
        rest = send_rest(0)
        if reach:
            pl.semaphore_wait(round_sem, 2)
        for _, there in hearts:
            pl.semaphore_signal(ready_sem, inc=1, device_id=there, device_id_type=MESH)
        for phase in range(PHASES):
            step = WIDE * phase
            sweep(step)
            wait_recv(edges)
            correct(
                step, [in_x.at[phase, side, 0] for side in range(2)],
                [in_y.at[phase, side, 0] for side in range(2)],
            )
            sweep(step + 1)
            wait_recv(rest)
            step_ring(phase)
            correct(
                step + 1, [ring_x.at[phase, side] for side in range(2)],
                [ring_y.at[phase, side] for side in range(2)],
            )
            if phase + 1 < PHASES:
                wait_send(edges + rest)
                edges = send_edges(phase + 1)
                rest = send_rest(phase + 1)

        wait_whole(rows_in, row_sem.at[0, 1])
        wait_whole(lines_in, row_sem.at[1, 1])
        wait_send(edges + rest)

    torso()


def main_kernel(n_slab, n_col, heart_refs, torso_refs, *refs):
    vol, line, dest, target, state, fields, rows_in, lines_in, *scratch = refs
    own_heart, own_torso = scratch[:heart_refs], scratch[heart_refs : heart_refs + torso_refs]
    meta_sem, send_sem, recv_sem, row_sem, ready_sem, round_sem = scratch[heart_refs + torso_refs :]
    place_ = Place(n_slab, n_col, vol.shape)

    @pl.when(place_.sec == 0)
    def _():
        heart_part(
            place_, vol, line, dest, target, state, rows_in, lines_in, *own_heart,
            meta_sem, send_sem, recv_sem, row_sem, ready_sem,
        )

    @pl.when(place_.sec == 1)
    def _():
        torso_part(
            place_, vol, fields, rows_in, lines_in, *own_torso,
            send_sem, recv_sem, row_sem, ready_sem, round_sem,
        )


def result_kernel(n_slab, state, fields, rows, lines, out, inflow_ref, sems):
    nx, ny, nz = state.shape[1:]
    tx = SEGMENTS * nx
    sec = lax.axis_index("sec")

    def heart():
        load(state, out.at[0], sems.at[0]).wait()

    def torso():
        copies = [
            load(fields.at[f], out.at[0, pl.ds(SEGMENTS * f, SEGMENTS)], sems.at[f])
            for f in range(3)
        ]
        slots = (n_slab, CAP * n_slab)
        goal = jnp.where(iota(slots, 1) < n_slab, lines[:, 0, 0:1], lines[:, 0, 1:2])
        marks = jnp.where(iota(slots, 0) == iota(slots, 1) % n_slab, goal, 0.0)
        marks = jnp.sum(marks, axis=0, keepdims=True)
        goals = iota((tx * ny, CAP * n_slab), 0).astype(jnp.float32)
        hits = (goals == marks).astype(jnp.float32).astype(jnp.bfloat16)
        got = jnp.concatenate(
            [
                jnp.concatenate([rows[:, 2 * r + h, :] for r in range(CAP)], axis=0)
                for h in range(2)
            ],
            axis=1,
        )
        inflow = matmul(jnp.concatenate([hits, hits], axis=1), split_halves(got), ((1,), (0,)))
        inflow_ref[...] = inflow.reshape(SEGMENTS, nx, ny, nz)
        copies.append(load(inflow_ref, out.at[0, pl.ds(3 * SEGMENTS, SEGMENTS)], sems.at[3]))
        for copy in copies:
            copy.wait()

    pl.when(sec == 0)(heart)
    pl.when(sec == 1)(torso)


def solution(mesh):
    n_slab, n_col = mesh.shape["slab"], mesh.shape["col"]

    def on_device(volume, epi_line, epi_dest, epi_target):
        _, fields, nx, ny, nz = volume.shape
        epi = epi_line.shape[-1]
        tx = SEGMENTS * nx
        f32, dma = jnp.float32, pltpu.SemaphoreType.DMA
        volume, epi_line, epi_dest, epi_target = (
            pltpu.with_memory_space_constraint(x, pltpu.HBM)
            for x in (volume, epi_line, epi_dest.reshape(epi_line.shape), epi_target)
        )
        hbm = pl.BlockSpec(memory_space=pltpu.HBM)
        vmem = pl.BlockSpec(memory_space=pltpu.VMEM)
        heart_scratch = [
                pltpu.VMEM((STEPS + 1, nx, ny, nz), f32),
                pltpu.VMEM((2, nx, ny, nz), f32),
                pltpu.VMEM((PHASES, 2, 5, ny, nz), f32),
                pltpu.VMEM((PHASES, 2, 5, nx, nz), f32),
                pltpu.VMEM((PHASES, 4, 1, nz), f32),
                pltpu.VMEM((PHASES, 2, 5, ny, nz), f32),
                pltpu.VMEM((PHASES, 2, 5, nx, nz), f32),
                pltpu.VMEM((PHASES, 4, 1, nz), f32),
                pltpu.VMEM((PHASES, 4, ny, nz), f32),
                pltpu.VMEM((4 * n_slab, 4 * nx * ny), jnp.bfloat16),
                pltpu.VMEM((3, 1, epi), jnp.int32),
                pltpu.VMEM((n_slab, 4, LANES), f32),
                pltpu.VMEM((n_slab, 1, NARROW), f32),
        ]
        torso_scratch = [
                pltpu.VMEM((STEPS + 1, SEGMENTS, nx, ny, nz), f32),
                pltpu.VMEM((SEGMENTS, nx, ny, nz), f32),
                pltpu.VMEM((SEGMENTS, nx, ny, nz), f32),
                pltpu.VMEM((PHASES, 2, 4, ny, nz), f32),
                pltpu.VMEM((PHASES, 2, 4, tx, nz), f32),
                pltpu.VMEM((PHASES, 4, 1, nz), f32),
                pltpu.VMEM((PHASES, 2, 4, ny, nz), f32),
                pltpu.VMEM((PHASES, 2, 4, tx, nz), f32),
                pltpu.VMEM((PHASES, 4, 1, nz), f32),
                pltpu.VMEM((PHASES, 2, ny, nz), f32),
                pltpu.VMEM((PHASES, 2, tx, nz), f32),
        ]
        regular = pltpu.SemaphoreType.REGULAR
        state, fields, rows, lines = pl.pallas_call(
            functools.partial(
                main_kernel, n_slab, n_col, len(heart_scratch), len(torso_scratch)
            ),
            out_shape=(
                jax.ShapeDtypeStruct((fields, nx, ny, nz), f32),
                jax.ShapeDtypeStruct((3, SEGMENTS, nx, ny, nz), f32),
                jax.ShapeDtypeStruct((n_slab, 4, LANES), f32),
                jax.ShapeDtypeStruct((n_slab, 1, NARROW), f32),
            ),
            in_specs=[hbm] * 4,
            out_specs=(vmem,) * 4,
            scratch_shapes=[
                *heart_scratch, *torso_scratch,
                dma((3,)), dma((12,)), dma((PHASES, 12)), dma((2, 2)), regular, regular,
            ],
            compiler_params=pltpu.CompilerParams(
                collective_id=0, has_side_effects=True, vmem_limit_bytes=VMEM_LIMIT
            ),
        )(volume, epi_line, epi_dest, epi_target)
        return pl.pallas_call(
            functools.partial(result_kernel, n_slab),
            out_shape=jax.ShapeDtypeStruct(volume.shape, f32),
            in_specs=[vmem, vmem, vmem, vmem],
            out_specs=hbm,
            scratch_shapes=[pltpu.VMEM((SEGMENTS, nx, ny, nz), f32), dma((4,))],
            compiler_params=pltpu.CompilerParams(vmem_limit_bytes=VMEM_LIMIT),
        )(state, fields, rows, lines)

    return jax.shard_map(
        on_device,
        mesh=mesh,
        in_specs=(
            P("sec", None, "slab", "col", None),
            P("slab", "col", None),
            P("slab", "col", None, None),
            P("slab", "col", None),
        ),
        out_specs=P("sec", None, "slab", "col", None),
        check_vma=False,
    )
```

```python
import functools

import jax
import jax.numpy as jnp
import numpy as np
from jax import lax
from jax.experimental import pallas as pl
from jax.experimental.pallas import tpu as pltpu
from jax.sharding import PartitionSpec as P

STEPS = 4
CAP = 2
GATES = 18
LANES = 128
NARROW = 8
SEGMENTS = 5
N_RING = 4
WIDE = 2
PHASES = STEPS // WIDE
VMEM_LIMIT = 24 * 1024 * 1024
MESH = pl.DeviceIdType.MESH

gate_half = np.linspace(-1.5, 1.5, GATES)
gate_slope = 0.3 + 0.1 * (np.arange(GATES) % 4)
gate_decay = np.exp(-1.0 / (2.0 * 30.0 ** (np.arange(GATES) / 17.0)))
gate_conduct = 0.02 + 0.01 * (np.arange(GATES) % 3)
gate_reversal = np.linspace(-1.0, 1.0, GATES)
relax_omega = 1.5625


def iota(shape, dim):
    return lax.broadcasted_iota(jnp.int32, shape, dim)


def split_halves(x):
    high = x.astype(jnp.bfloat16)
    low = (x - high.astype(jnp.float32)).astype(jnp.bfloat16)
    return jnp.concatenate([high, low], axis=0)


def matmul(a, b, contract):
    return lax.dot_general(
        a, b, (contract, ((), ())), preferred_element_type=jnp.float32
    )


class Place:
    def __init__(self, n_slab, n_col, sizes):
        self.n_slab, self.n_col = n_slab, n_col
        self.ring_size = n_slab // N_RING
        self.sec = sec = lax.axis_index("sec")
        self.slab = slab = lax.axis_index("slab")
        self.col = col = lax.axis_index("col")
        _, _, nx, self.ny, self.nz = sizes
        plane = (self.ny, self.nz)
        self.sub, self.lane = iota(plane, 0), iota(plane, 1)
        self.exists = exists = ((slab > 0, slab < n_slab - 1), (col > 0, col < n_col - 1))
        self.low_y = jnp.logical_and(self.sub == 0, exists[1][0])
        self.high_y = jnp.logical_and(self.sub == self.ny - 1, exists[1][1])
        moves = [(i, j) for i in range(2) for j in range(2)]
        self.met = [
            (jnp.logical_and(exists[0][i], exists[1][j]), (sec, slab + 2 * i - 1, col + 2 * j - 1))
            for i, j in moves
        ]
        self.met += [(exists[0][i], (sec, slab + 2 * i - 1, col)) for i in range(2)]
        self.met += [(exists[1][j], (sec, slab, col + 2 * j - 1)) for j in range(2)]

    def across(self, sec):
        return [
            (self.slab >= 0, (sec, lax.rem(self.slab + i * self.ring_size, self.n_slab), self.col))
            for i in range(N_RING)
        ]

    def greet(self, others):
        for here, there in self.met[4:] + others + self.met[:4]:

            @pl.when(here)
            def _(there=there):
                pl.semaphore_signal(
                    pltpu.get_barrier_semaphore(), inc=1, device_id=there, device_id_type=MESH
                )

    def await_met(self, others=()):
        count = sum(here.astype(jnp.int32) for here, _ in [*self.met, *others])
        pl.semaphore_wait(pltpu.get_barrier_semaphore(), count)

    def exchange(self, phase, parts, send_sem, recv_sem):
        copies = []
        for way, (direction, src, dst) in parts:
            here, there = self.met[direction]
            copy = pltpu.make_async_remote_copy(
                src_ref=src, dst_ref=dst, send_sem=send_sem.at[way],
                recv_sem=recv_sem.at[phase, way], device_id=there, device_id_type=MESH,
            )
            copies.append((here, copy, self.met[(3, 2, 1, 0, 5, 4, 7, 6)[direction]][0]))
        return copies

    def edges(self, phase, out_x, out_y, in_x, in_y, first, count):
        fields = pl.ds(first, count)
        return [
            (4 + 2 * axis + side, out.at[phase, side, fields], into.at[phase, 1 - side, fields])
            for axis, (out, into) in enumerate(((out_x, in_x), (out_y, in_y)))
            for side in range(2)
        ]

    def corners(self, phase, out_c, in_c):
        return [(c, out_c.at[phase, c], in_c.at[phase, 3 - c]) for c in range(4)]

    def beside_lines(self, cells, low, high):
        last = self.ny - 1
        below = jnp.where(self.sub == 0, low, pltpu.roll(cells, 1, 0))
        return below + jnp.where(self.sub == last, high, pltpu.roll(cells, last, 0))

    def beside_z(self, cells, low, high):
        last = self.nz - 1
        below = jnp.where(self.lane == 0, low, pltpu.roll(cells, 1, 1))
        return below + jnp.where(self.lane == last, high, pltpu.roll(cells, last, 1))


def start(copies):
    for here, copy, _ in copies:
        pl.when(here)(copy.start)


def wait_recv(copies):
    for _, copy, here in copies:
        pl.when(here)(copy.wait_recv)


def wait_send(copies):
    for here, copy, _ in copies:
        pl.when(here)(copy.wait_send)


def load(src, dst, sem):
    copy = pltpu.make_async_copy(src, dst, sem)
    copy.start()
    return copy


def wait_whole(ref, sem):
    pltpu.make_async_copy(ref, ref, sem).wait()


def heart_part(
    place_, vol, line_hbm, dest_hbm, target_hbm, state, rows_in, lines_in,
    pots, moments, out_x, out_y, out_c, in_x, in_y, in_c, ring, picks, meta, rows_out, lines_out,
    meta_sem, send_sem, recv_sem, row_sem, ready_sem,
):
    n_slab, slab, col = place_.n_slab, place_.slab, place_.col
    low_y, high_y = place_.low_y, place_.high_y
    nx, ny, nz = vol.shape[2:]
    ends_x, ends_y = (0, nx - 1), (0, ny - 1)

    def bends(volts):
        scaled = {}
        for j in range(GATES):
            slope = float(0.5 / gate_slope[j])
            if slope not in scaled:
                scaled[slope] = volts * slope
            yield j, jnp.tanh(scaled[slope] - float(gate_half[j] * slope))

    def step_plane(step, x, with_moments):
        volts = pots[step, x]
        sigma = state[GATES + 1, x]
        beside_x = pots[step, jnp.maximum(x - 1, 0)] + pots[step, jnp.minimum(x + 1, nx - 1)]
        around = place_.beside_lines(volts, volts, volts)
        around += place_.beside_z(volts, volts, volts)
        flux = 0.12 * (beside_x - 2.0 * volts) + 0.04 * (around - 4.0 * volts)
        sums, weighted = {}, {}
        later, later_weighted = 0.0, 0.0
        for j, bend in bends(volts):
            rest = float(0.5 * (1.0 - gate_decay[j]))
            gate = state[1 + j, x] * float(gate_decay[j]) + (rest * bend + rest)
            state[1 + j, x] = gate
            conduct = float(gate_conduct[j])
            drawn = gate * float(gate_reversal[j])
            if conduct in sums:
                sums[conduct] += gate
                weighted[conduct] += drawn
            else:
                sums[conduct], weighted[conduct] = gate, drawn
            if with_moments:
                later += gate * float(gate_conduct[j] * gate_decay[j])
                later_weighted += drawn * float(gate_conduct[j] * gate_decay[j])
        if with_moments:
            moments[0, x] = later
            moments[1, x] = later_weighted
        current = sum(c * (volts * sums[c] - weighted[c]) for c in sums)
        pots[step + 1, x] = volts + sigma * flux - current

    def first_moments(x, _):
        later, later_weighted = 0.0, 0.0
        for j in range(GATES):
            part = state[1 + j, x] * float(gate_conduct[j] * gate_decay[j])
            later += part
            later_weighted += part * float(gate_reversal[j])
        moments[0, x] = later
        moments[1, x] = later_weighted
        return 0

    def send_edges(phase):
        step = WIDE * phase
        for side in range(2):
            out_x[phase, side, 0] = pots[step, ends_x[side]]
            for x in range(nx):
                y = ends_y[side]
                out_y[phase, side, 0, x : x + 1, :] = pots[step, x, y : y + 1, :]
        parts = place_.edges(phase, out_x, out_y, in_x, in_y, 0, 1)
        copies = place_.exchange(phase, list(enumerate(parts)), send_sem, recv_sem)
        start(copies)
        return copies

    def send_rest(phase):
        step = WIDE * phase
        for side in range(2):
            x = ends_x[side]
            out_x[phase, side, 1] = pots[step, x + 1 - 2 * side]
            out_x[phase, side, 2] = moments[0, x]
            out_x[phase, side, 3] = moments[1, x]
            if phase == 0:
                out_x[phase, side, 4] = state[GATES + 1, x]
            for j, y in enumerate(ends_y):
                out_c[phase, 2 * side + j] = pots[step, x, y : y + 1, :]
        for x in range(nx):
            for side, y in enumerate(ends_y):
                inward = y + 1 - 2 * side
                rows = [pots[step, x, inward : inward + 1, :]]
                rows += [moments[f, x, y : y + 1, :] for f in range(2)]
                if phase == 0:
                    rows.append(state[GATES + 1, x, y : y + 1, :])
                for f, row in enumerate(rows):
                    out_y[phase, side, 1 + f, x : x + 1, :] = row
        parts = place_.edges(phase, out_x, out_y, in_x, in_y, 1, 4 if phase == 0 else 3)
        parts += place_.corners(phase, out_c, in_c)
        copies = place_.exchange(phase, list(enumerate(parts, 4)), send_sem, recv_sem)
        start(copies)
        return copies

    def correct(step, planes, rows):
        for side, x in enumerate(ends_x):
            beyond = jnp.where(place_.exists[0][side], planes[side][...] - pots[step, x], 0.0)
            pots[step + 1, x] += 0.12 * state[GATES + 1, x] * beyond
        for x in range(nx):
            volts = pots[step, x]
            beyond = jnp.where(low_y, rows[0][x : x + 1, :] - volts, 0.0)
            beyond += jnp.where(high_y, rows[1][x : x + 1, :] - volts, 0.0)
            pots[step + 1, x] += 0.04 * state[GATES + 1, x] * beyond

    def step_ring(phase):
        step = WIDE * phase
        for axis, (into, across, along) in enumerate(((in_x, 0.12, 0.04), (in_y, 0.04, 0.12))):
            for side in range(2):
                volts, far = into[phase, side, 0], into[phase, side, 1]
                near = pots[step, ends_x[side]] if axis == 0 else out_y[phase, side, 0]
                tips = []
                for end in range(2):
                    corner = in_c[phase, 2 * side + end if axis == 0 else 2 * end + side]
                    own = volts[ends_y[end] : ends_y[end] + 1]
                    tips.append(jnp.where(place_.exists[1 - axis][end], corner, own))
                flux = across * (near + far - 2.0 * volts)
                flux += along * (place_.beside_lines(volts, *tips) - 2.0 * volts)
                flux += 0.04 * (place_.beside_z(volts, volts, volts) - 2.0 * volts)
                gain = np.float64(0.5) * gate_conduct * (1.0 - gate_decay)
                drawn, weighted = 0.0, 0.0
                for j, bend in bends(volts):
                    drawn += bend * float(gain[j])
                    weighted += bend * float(gain[j] * gate_reversal[j])
                drawn += into[phase, side, 2] + float(gain.sum())
                weighted += into[phase, side, 3] + float((gain * gate_reversal).sum())
                fresh = volts + in_sigma(axis, side) * flux - (volts * drawn - weighted)
                ring[phase, 2 * axis + side] = fresh

    def in_sigma(axis, side):
        return (in_x, in_y)[axis][0, side, 4]

    def to_all(src, dst, which):
        def send(i, _):
            there = place_.ring_size * lax.rem(i, N_RING) + i // N_RING
            pltpu.make_async_remote_copy(
                src_ref=src.at[there], dst_ref=dst.at[slab], send_sem=row_sem.at[which, 0],
                recv_sem=row_sem.at[which, 1], device_id=(1, there, col), device_id_type=MESH,
            ).start()
            return 0

        lax.fori_loop(0, n_slab, send, 0)

    def heart():
        loads = [
            load(vol.at[0, 0], pots.at[0], send_sem.at[4]),
            load(vol.at[0, pl.ds(1, GATES + 1)], state.at[pl.ds(1, GATES + 1)], send_sem.at[5]),
        ]
        metas = [
            load(src.at[0], meta.at[i], meta_sem.at[i])
            for i, src in enumerate((line_hbm, dest_hbm, target_hbm))
        ]
        place_.greet(place_.across(1))
        loads[0].wait()
        place_.await_met()
        edges = send_edges(0)
        loads[1].wait()
        lax.fori_loop(0, nx, first_moments, 0, unroll=2)
        rest = send_rest(0)

        for copy in metas:
            copy.wait()
        lines = nx * ny
        fill_picks(lines)
        for phase in range(PHASES):
            step = WIDE * phase

            def first(x, _):
                step_plane(step, x, False)
                return 0

            def second(x, _):
                step_plane(step + 1, x, phase + 1 < PHASES)
                return 0

            lax.fori_loop(0, nx, first, 0, unroll=2)
            if phase + 1 == PHASES:
                pl.semaphore_wait(ready_sem, N_RING)
                to_all(lines_out, lines_in, 1)
            wait_recv(edges)
            correct(
                step, [in_x.at[phase, side, 0] for side in range(2)],
                [in_y.at[phase, side, 0] for side in range(2)],
            )
            lax.fori_loop(0, nx, second, 0, unroll=2)
            wait_recv(rest)
            step_ring(phase)
            correct(
                step + 1, [ring.at[phase, side] for side in range(2)],
                [ring.at[phase, 2 + side] for side in range(2)],
            )
            if phase + 1 < PHASES:
                wait_send(edges + rest)
                edges = send_edges(phase + 1)
                rest = send_rest(phase + 1)

        state[0] = pots[STEPS]
        final = pots[STEPS].reshape(lines, nz)
        source = jnp.concatenate([final[:, :LANES], final[:, LANES:]], axis=0)
        rows = matmul(picks[...], split_halves(source), ((1,), (0,)))
        rows_out[...] = rows.reshape(n_slab, 4, LANES)
        to_all(rows_out, rows_in, 0)
        wait_whole(rows_out, row_sem.at[0, 0])
        wait_whole(lines_out, row_sem.at[1, 0])
        wait_send(edges + rest)

    def fill_picks(lines):
        epi = meta.shape[2]
        line, dest, target = meta[0], meta[1], meta[2]
        slots = 4 * n_slab
        own = iota((slots, epi), 0)
        marks = own // 4 == dest
        before = (iota((epi, epi), 0) < iota((epi, epi), 1)).astype(jnp.bfloat16)
        rank = matmul(marks.astype(jnp.float32).astype(jnp.bfloat16), before, ((1,), (0,)))
        wanted = ((own // 2) % 2).astype(jnp.float32)
        place = jnp.logical_and(marks, rank == wanted)
        half = (own % 2).astype(jnp.float32)
        place = place.astype(jnp.float32)
        places = jnp.concatenate([place * (1.0 - half), place * half], axis=1)
        held = (iota((lines, epi), 0) == line).astype(jnp.float32).astype(jnp.bfloat16)
        for h in range(2):
            part = matmul(
                places[:, h * epi : (h + 1) * epi].astype(jnp.bfloat16), held, ((1,), (1,))
            ).astype(jnp.bfloat16)
            picks[:, h * lines : (h + 1) * lines] = part
            picks[:, (h + 2) * lines : (h + 3) * lines] = part
        own_d = iota((n_slab, epi), 0)
        marks_d = own_d == dest
        rank_d = matmul(marks_d.astype(jnp.float32).astype(jnp.bfloat16), before, ((1,), (0,)))
        goals = []
        for r in range(CAP):
            chosen = jnp.logical_and(marks_d, rank_d == float(r))
            goal = jnp.where(chosen, (target + 1).astype(jnp.float32), 0.0)
            goals.append(jnp.sum(goal, axis=1, keepdims=True) - 1.0)
        lines_out[:, 0, :] = jnp.where(iota((n_slab, NARROW), 1) == 0, goals[0], goals[1])

    heart()


def torso_part(
    place_, vol, out, rows_in, hits_ref, lines_in,
    pots, coef, drive, out_x, out_y, out_c, in_x, in_y, in_c, ring_x, ring_y,
    send_sem, recv_sem, row_sem, ready_sem,
):
    n_slab, slab, col = place_.n_slab, place_.slab, place_.col
    low_y, high_y = place_.low_y, place_.high_y
    nx, ny, nz = vol.shape[2:]
    tx = SEGMENTS * nx
    ends = ((0, 0), (SEGMENTS - 1, nx - 1))
    before_last = 1.0 - relax_omega

    def field(f):
        return vol.at[0, pl.ds(SEGMENTS * f, SEGMENTS)]

    def before(step):
        return pots.at[step - 1] if step else out.at[1]

    def coefficients(k, _):
        for r in range(nx):
            gain = relax_omega / (6.0 + out[2, k, r])
            coef[k, r] = gain
            drive[k, r] = gain * drive[k, r]
        return 0

    def send_edges(phase):
        step = WIDE * phase
        for side, (k, r) in enumerate(ends):
            out_x[phase, side, 0] = pots[step, k, r]

        def pack(k, _):
            for r in range(nx):
                for side, y in enumerate((0, ny - 1)):
                    row = pots[step, k, r, y : y + 1, :]
                    out_y[phase, side, 0, pl.ds(k * nx + r, 1), :] = row
            return 0

        lax.fori_loop(0, SEGMENTS, pack, 0)
        parts = place_.edges(phase, out_x, out_y, in_x, in_y, 0, 1)
        copies = place_.exchange(phase, list(enumerate(parts)), send_sem, recv_sem)
        start(copies)
        return copies

    def send_rest(phase):
        step = WIDE * phase
        old = before(step)
        for side, (k, r) in enumerate(ends):
            out_x[phase, side, 1] = pots[step, k, r + 1 - 2 * side]
            out_x[phase, side, 2] = before_last * old[k, r] + drive[k, r]
            if phase == 0:
                out_x[phase, side, 3] = coef[k, r]
            for j, y in enumerate((0, ny - 1)):
                out_c[phase, 2 * side + j] = pots[step, k, r, y : y + 1, :]

        def pack(k, _):
            for r in range(nx):
                added = before_last * old[k, r] + drive[k, r]
                for side, y in enumerate((0, ny - 1)):
                    inward = y + 1 - 2 * side
                    rows = [pots[step, k, r, inward : inward + 1, :], added[y : y + 1]]
                    if phase == 0:
                        rows.append(coef[k, r, y : y + 1, :])
                    for f, row in enumerate(rows):
                        out_y[phase, side, 1 + f, pl.ds(k * nx + r, 1), :] = row
            return 0

        lax.fori_loop(0, SEGMENTS, pack, 0)
        parts = place_.edges(phase, out_x, out_y, in_x, in_y, 1, 3 if phase == 0 else 2)
        parts += place_.corners(phase, out_c, in_c)
        copies = place_.exchange(phase, list(enumerate(parts, 4)), send_sem, recv_sem)
        start(copies)
        return copies

    def sweep(step):
        old = before(step)

        def segment(k, _):
            planes = [pots[step, k, r] for r in range(nx)]
            below = jnp.where(k > 0, pots[step, jnp.maximum(k - 1, 0), nx - 1], 0.0)
            above = jnp.where(
                k < SEGMENTS - 1, pots[step, jnp.minimum(k + 1, SEGMENTS - 1), 0], 0.0
            )
            around = [below] + planes + [above]
            for r in range(nx):
                beside = around[r] + around[r + 2]
                beside += place_.beside_lines(planes[r], 0.0, 0.0)
                beside += place_.beside_z(planes[r], 0.0, 0.0)
                pots[step + 1, k, r] = drive[k, r] + before_last * old[k, r] + coef[k, r] * beside
            return 0

        lax.fori_loop(0, SEGMENTS, segment, 0)

    def correct(step, planes, rows):
        for side, (k, r) in enumerate(ends):
            beyond = jnp.where(place_.exists[0][side], planes[side][...], 0.0)
            pots[step + 1, k, r] += coef[k, r] * beyond

        def segment(k, _):
            low, high = (face[pl.ds(k * nx, nx), :] for face in rows)
            for r in range(nx):
                beyond = jnp.where(low_y, low[r : r + 1], 0.0)
                beyond += jnp.where(high_y, high[r : r + 1], 0.0)
                fresh = pots[step + 1, k, r] + coef[k, r] * beyond
                pots[step + 1, k, r] = fresh
                if step + 2 == STEPS:
                    out[1, k, r] = fresh
                if step + 1 == STEPS:
                    out[0, k, r] = fresh
            return 0

        lax.fori_loop(0, SEGMENTS, segment, 0)

    def step_ring(phase):
        step = WIDE * phase
        for side in range(2):
            cells = in_x[phase, side, 0]
            tips = [
                jnp.where(place_.exists[1][end], in_c[phase, 2 * side + end], 0.0)
                for end in range(2)
            ]
            beside = pots[step, *ends[side]] + in_x[phase, side, 1]
            beside += place_.beside_lines(cells, *tips) + place_.beside_z(cells, 0.0, 0.0)
            ring_x[phase, side] = in_x[phase, side, 2] + in_x[0, side, 3] * beside
        for side in range(2):
            tips = [
                jnp.where(place_.exists[0][end], in_c[phase, 2 * end + side], 0.0)
                for end in range(2)
            ]
            for k in range(SEGMENTS):
                rows = pl.ds(k * nx, nx)
                cells = in_y[phase, side, 0, rows, :]
                low = in_y[phase, side, 0, k * nx - 1 : k * nx, :] if k else tips[0]
                high = tips[1]
                if k + 1 < SEGMENTS:
                    high = in_y[phase, side, 0, (k + 1) * nx : (k + 1) * nx + 1, :]
                beside = out_y[phase, side, 0, rows, :] + in_y[phase, side, 1, rows, :]
                beside += place_.beside_lines(cells, low, high) + place_.beside_z(cells, 0.0, 0.0)
                ring_y[phase, side, rows, :] = (
                    in_y[phase, side, 2, rows, :] + in_y[0, side, 3, rows, :] * beside
                )

    def torso():
        loads = [
            load(field(0), pots.at[0], send_sem.at[4]),
            load(field(2), out.at[2], send_sem.at[5]),
            load(field(3), drive, send_sem.at[6]),
            load(field(1), out.at[1], send_sem.at[7]),
        ]
        ring_size = place_.ring_size
        at = lax.rem(slab, ring_size)

        def along(k):
            return (1, slab - at + lax.rem(at + k + ring_size, ring_size), col)

        others = []
        if ring_size > 2:
            others += [(at == 0, along(-1)), (at == ring_size - 1, along(1))]
        for k in sorted(range(2, ring_size - 1), key=lambda k: -min(k, ring_size - k)):
            others.append((slab >= 0, along(k)))
        place_.greet(others)

        hearts = place_.across(0)
        place_.await_met(others + hearts)
        for _, there in hearts:
            pl.semaphore_signal(ready_sem, inc=1, device_id=there, device_id_type=MESH)
        loads[0].wait()
        edges = send_edges(0)
        for copy in loads[1:]:
            copy.wait()
        lax.fori_loop(0, SEGMENTS, coefficients, 0)
        rest = send_rest(0)
        for phase in range(PHASES):
            step = WIDE * phase
            sweep(step)
            wait_recv(edges)
            correct(
                step, [in_x.at[phase, side, 0] for side in range(2)],
                [in_y.at[phase, side, 0] for side in range(2)],
            )
            sweep(step + 1)
            wait_recv(rest)
            step_ring(phase)
            correct(
                step + 1, [ring_x.at[phase, side] for side in range(2)],
                [ring_y.at[phase, side] for side in range(2)],
            )
            if phase + 1 < PHASES:
                wait_send(edges + rest)
                edges = send_edges(phase + 1)
                rest = send_rest(phase + 1)

        wait_whole(lines_in, row_sem.at[1, 1])
        slots = (n_slab, CAP * n_slab)
        goal = jnp.where(iota(slots, 1) < n_slab, lines_in[:, 0, 0:1], lines_in[:, 0, 1:2])
        marks = jnp.where(iota(slots, 0) == iota(slots, 1) % n_slab, goal, 0.0)
        marks = jnp.sum(marks, axis=0, keepdims=True)
        goals = iota((tx * ny, CAP * n_slab), 0).astype(jnp.float32)
        hits = (goals == marks).astype(jnp.float32).astype(jnp.bfloat16)
        hits_ref[:, : CAP * n_slab] = hits
        hits_ref[:, CAP * n_slab :] = hits
        wait_whole(rows_in, row_sem.at[0, 1])
        wait_send(edges + rest)

    torso()


def main_kernel(n_slab, n_col, heart_refs, torso_refs, *refs):
    vol, line, dest, target, state, fields, rows_in, hits, lines_in, *scratch = refs
    own_heart, own_torso = scratch[:heart_refs], scratch[heart_refs : heart_refs + torso_refs]
    meta_sem, send_sem, recv_sem, row_sem, ready_sem = scratch[heart_refs + torso_refs :]
    place_ = Place(n_slab, n_col, vol.shape)

    @pl.when(place_.sec == 0)
    def _():
        heart_part(
            place_, vol, line, dest, target, state, rows_in, lines_in, *own_heart,
            meta_sem, send_sem, recv_sem, row_sem, ready_sem,
        )

    @pl.when(place_.sec == 1)
    def _():
        torso_part(
            place_, vol, fields, rows_in, hits, lines_in, *own_torso,
            send_sem, recv_sem, row_sem, ready_sem,
        )


def result_kernel(state, fields, rows, hits, out, inflow_ref, sems):
    nx, ny, nz = state.shape[1:]
    tx = SEGMENTS * nx
    sec = lax.axis_index("sec")

    def heart():
        load(state, out.at[0], sems.at[0]).wait()

    def torso():
        copies = [
            load(fields.at[f], out.at[0, pl.ds(SEGMENTS * f, SEGMENTS)], sems.at[f])
            for f in range(3)
        ]
        got = jnp.concatenate(
            [
                jnp.concatenate([rows[:, 2 * r + h, :] for r in range(CAP)], axis=0)
                for h in range(2)
            ],
            axis=1,
        )
        inflow = matmul(hits[...], split_halves(got), ((1,), (0,)))
        inflow_ref[...] = inflow.reshape(SEGMENTS, nx, ny, nz)
        copies.append(load(inflow_ref, out.at[0, pl.ds(3 * SEGMENTS, SEGMENTS)], sems.at[3]))
        for copy in copies:
            copy.wait()

    pl.when(sec == 0)(heart)
    pl.when(sec == 1)(torso)


def solution(mesh):
    n_slab, n_col = mesh.shape["slab"], mesh.shape["col"]

    def on_device(volume, epi_line, epi_dest, epi_target):
        _, fields, nx, ny, nz = volume.shape
        epi = epi_line.shape[-1]
        tx = SEGMENTS * nx
        f32, dma = jnp.float32, pltpu.SemaphoreType.DMA
        volume, epi_line, epi_dest, epi_target = (
            pltpu.with_memory_space_constraint(x, pltpu.HBM)
            for x in (volume, epi_line, epi_dest.reshape(epi_line.shape), epi_target)
        )
        hbm = pl.BlockSpec(memory_space=pltpu.HBM)
        vmem = pl.BlockSpec(memory_space=pltpu.VMEM)
        heart_scratch = [
                pltpu.VMEM((STEPS + 1, nx, ny, nz), f32),
                pltpu.VMEM((2, nx, ny, nz), f32),
                pltpu.VMEM((PHASES, 2, 5, ny, nz), f32),
                pltpu.VMEM((PHASES, 2, 5, nx, nz), f32),
                pltpu.VMEM((PHASES, 4, 1, nz), f32),
                pltpu.VMEM((PHASES, 2, 5, ny, nz), f32),
                pltpu.VMEM((PHASES, 2, 5, nx, nz), f32),
                pltpu.VMEM((PHASES, 4, 1, nz), f32),
                pltpu.VMEM((PHASES, 4, ny, nz), f32),
                pltpu.VMEM((4 * n_slab, 4 * nx * ny), jnp.bfloat16),
                pltpu.VMEM((3, 1, epi), jnp.int32),
                pltpu.VMEM((n_slab, 4, LANES), f32),
                pltpu.VMEM((n_slab, 1, NARROW), f32),
        ]
        torso_scratch = [
                pltpu.VMEM((STEPS + 1, SEGMENTS, nx, ny, nz), f32),
                pltpu.VMEM((SEGMENTS, nx, ny, nz), f32),
                pltpu.VMEM((SEGMENTS, nx, ny, nz), f32),
                pltpu.VMEM((PHASES, 2, 4, ny, nz), f32),
                pltpu.VMEM((PHASES, 2, 4, tx, nz), f32),
                pltpu.VMEM((PHASES, 4, 1, nz), f32),
                pltpu.VMEM((PHASES, 2, 4, ny, nz), f32),
                pltpu.VMEM((PHASES, 2, 4, tx, nz), f32),
                pltpu.VMEM((PHASES, 4, 1, nz), f32),
                pltpu.VMEM((PHASES, 2, ny, nz), f32),
                pltpu.VMEM((PHASES, 2, tx, nz), f32),
        ]
        regular = pltpu.SemaphoreType.REGULAR
        state, fields, rows, hits = pl.pallas_call(
            functools.partial(
                main_kernel, n_slab, n_col, len(heart_scratch), len(torso_scratch)
            ),
            out_shape=(
                jax.ShapeDtypeStruct((fields, nx, ny, nz), f32),
                jax.ShapeDtypeStruct((3, SEGMENTS, nx, ny, nz), f32),
                jax.ShapeDtypeStruct((n_slab, 4, LANES), f32),
                jax.ShapeDtypeStruct((tx * ny, 2 * CAP * n_slab), jnp.bfloat16),
            ),
            in_specs=[hbm] * 4,
            out_specs=(vmem,) * 4,
            scratch_shapes=[
                pltpu.VMEM((n_slab, 1, NARROW), f32),
                *heart_scratch, *torso_scratch,
                dma((3,)), dma((12,)), dma((PHASES, 12)), dma((2, 2)), regular,
            ],
            compiler_params=pltpu.CompilerParams(
                collective_id=0, has_side_effects=True, vmem_limit_bytes=VMEM_LIMIT
            ),
        )(volume, epi_line, epi_dest, epi_target)
        return pl.pallas_call(
            result_kernel,
            out_shape=jax.ShapeDtypeStruct(volume.shape, f32),
            in_specs=[vmem, vmem, vmem, vmem],
            out_specs=hbm,
            scratch_shapes=[pltpu.VMEM((SEGMENTS, nx, ny, nz), f32), dma((4,))],
            compiler_params=pltpu.CompilerParams(vmem_limit_bytes=VMEM_LIMIT),
        )(state, fields, rows, hits)

    return jax.shard_map(
        on_device,
        mesh=mesh,
        in_specs=(
            P("sec", None, "slab", "col", None),
            P("slab", "col", None),
            P("slab", "col", None, None),
            P("slab", "col", None),
        ),
        out_specs=P("sec", None, "slab", "col", None),
        check_vma=False,
    )
```

```python
import functools

import jax
import jax.numpy as jnp
import numpy as np
from jax import lax
from jax.experimental import pallas as pl
from jax.experimental.pallas import tpu as pltpu
from jax.sharding import PartitionSpec as P

STEPS = 4
CAP = 2
GATES = 18
PARTS = 3
CHUNK = GATES // PARTS
LANES = 128
NARROW = 8
SEGMENTS = 5
N_RING = 4
WIDE = 2
PHASES = STEPS // WIDE
VMEM_LIMIT = 24 * 1024 * 1024
MESH = pl.DeviceIdType.MESH

gate_half = np.linspace(-1.5, 1.5, GATES)
gate_slope = 0.3 + 0.1 * (np.arange(GATES) % 4)
gate_decay = np.exp(-1.0 / (2.0 * 30.0 ** (np.arange(GATES) / 17.0)))
gate_conduct = 0.02 + 0.01 * (np.arange(GATES) % 3)
gate_reversal = np.linspace(-1.0, 1.0, GATES)
relax_omega = 1.5625


def iota(shape, dim):
    return lax.broadcasted_iota(jnp.int32, shape, dim)


def split_halves(x):
    high = x.astype(jnp.bfloat16)
    low = (x - high.astype(jnp.float32)).astype(jnp.bfloat16)
    return jnp.concatenate([high, low], axis=0)


def matmul(a, b, contract):
    return lax.dot_general(
        a, b, (contract, ((), ())), preferred_element_type=jnp.float32
    )


class Place:
    def __init__(self, n_slab, n_col, sizes):
        self.n_slab, self.n_col = n_slab, n_col
        self.ring_size = n_slab // N_RING
        self.sec = sec = lax.axis_index("sec")
        self.slab = slab = lax.axis_index("slab")
        self.col = col = lax.axis_index("col")
        _, _, nx, self.ny, self.nz = sizes
        plane = (self.ny, self.nz)
        self.sub, self.lane = iota(plane, 0), iota(plane, 1)
        self.exists = exists = ((slab > 0, slab < n_slab - 1), (col > 0, col < n_col - 1))
        self.low_y = jnp.logical_and(self.sub == 0, exists[1][0])
        self.high_y = jnp.logical_and(self.sub == self.ny - 1, exists[1][1])
        moves = [(i, j) for i in range(2) for j in range(2)]
        self.met = [
            (jnp.logical_and(exists[0][i], exists[1][j]), (sec, slab + 2 * i - 1, col + 2 * j - 1))
            for i, j in moves
        ]
        self.met += [(exists[0][i], (sec, slab + 2 * i - 1, col)) for i in range(2)]
        self.met += [(exists[1][j], (sec, slab, col + 2 * j - 1)) for j in range(2)]

    def across(self, sec):
        return [
            (self.slab >= 0, (sec, lax.rem(self.slab + i * self.ring_size, self.n_slab), self.col))
            for i in range(N_RING)
        ]

    def greet(self, first=(), last=()):
        for here, there in [*self.met[4:], *first, *self.met[:4], *last]:

            @pl.when(here)
            def _(there=there):
                pl.semaphore_signal(
                    pltpu.get_barrier_semaphore(), inc=1, device_id=there, device_id_type=MESH
                )

    def await_met(self, others=()):
        count = sum(here.astype(jnp.int32) for here, _ in [*self.met, *others])
        pl.semaphore_wait(pltpu.get_barrier_semaphore(), count)

    def exchange(self, phase, parts, send_sem, recv_sem):
        copies = []
        for way, (direction, src, dst) in parts:
            here, there = self.met[direction]
            copy = pltpu.make_async_remote_copy(
                src_ref=src, dst_ref=dst, send_sem=send_sem.at[way],
                recv_sem=recv_sem.at[phase, way], device_id=there, device_id_type=MESH,
            )
            copies.append((here, copy, self.met[(3, 2, 1, 0, 5, 4, 7, 6)[direction]][0]))
        return copies

    def edges(self, phase, out_x, out_y, in_x, in_y, first, count):
        fields = pl.ds(first, count)
        return [
            (4 + 2 * axis + side, out.at[phase, side, fields], into.at[phase, 1 - side, fields])
            for axis, (out, into) in enumerate(((out_x, in_x), (out_y, in_y)))
            for side in range(2)
        ]

    def corners(self, phase, out_c, in_c):
        return [(c, out_c.at[phase, c], in_c.at[phase, 3 - c]) for c in range(4)]

    def beside_lines(self, cells, low, high):
        last = self.ny - 1
        below = jnp.where(self.sub == 0, low, pltpu.roll(cells, 1, 0))
        return below + jnp.where(self.sub == last, high, pltpu.roll(cells, last, 0))

    def beside_z(self, cells, low, high):
        last = self.nz - 1
        below = jnp.where(self.lane == 0, low, pltpu.roll(cells, 1, 1))
        return below + jnp.where(self.lane == last, high, pltpu.roll(cells, last, 1))


def start(copies):
    for here, copy, _ in copies:
        pl.when(here)(copy.start)


def wait_recv(copies):
    for _, copy, here in copies:
        pl.when(here)(copy.wait_recv)


def wait_send(copies):
    for here, copy, _ in copies:
        pl.when(here)(copy.wait_send)


def load(src, dst, sem):
    copy = pltpu.make_async_copy(src, dst, sem)
    copy.start()
    return copy


def wait_whole(ref, sem):
    pltpu.make_async_copy(ref, ref, sem).wait()


def heart_part(
    place_, vol, line_hbm, dest_hbm, target_hbm, state, rows_in, lines_in,
    pots, moments, out_x, out_y, out_c, in_x, in_y, in_c, ring, picks, meta, rows_out, lines_out,
    meta_sem, send_sem, recv_sem, row_sem, ready_sem,
):
    n_slab, slab, col = place_.n_slab, place_.slab, place_.col
    low_y, high_y = place_.low_y, place_.high_y
    nx, ny, nz = vol.shape[2:]
    ends_x, ends_y = (0, nx - 1), (0, ny - 1)

    def bends(volts):
        scaled = {}
        for j in range(GATES):
            slope = float(0.5 / gate_slope[j])
            if slope not in scaled:
                scaled[slope] = volts * slope
            yield j, jnp.tanh(scaled[slope] - float(gate_half[j] * slope))

    def step_plane(step, x, with_moments):
        volts = pots[step, x]
        sigma = state[GATES + 1, x]
        beside_x = pots[step, jnp.maximum(x - 1, 0)] + pots[step, jnp.minimum(x + 1, nx - 1)]
        around = place_.beside_lines(volts, volts, volts)
        around += place_.beside_z(volts, volts, volts)
        flux = 0.12 * (beside_x - 2.0 * volts) + 0.04 * (around - 4.0 * volts)
        sums, weighted = {}, {}
        later, later_weighted = 0.0, 0.0
        for j, bend in bends(volts):
            rest = float(0.5 * (1.0 - gate_decay[j]))
            gate = state[1 + j, x] * float(gate_decay[j]) + (rest * bend + rest)
            state[1 + j, x] = gate
            conduct = float(gate_conduct[j])
            drawn = gate * float(gate_reversal[j])
            if conduct in sums:
                sums[conduct] += gate
                weighted[conduct] += drawn
            else:
                sums[conduct], weighted[conduct] = gate, drawn
            if with_moments:
                later += gate * float(gate_conduct[j] * gate_decay[j])
                later_weighted += drawn * float(gate_conduct[j] * gate_decay[j])
        if with_moments:
            moments[0, x] = later
            moments[1, x] = later_weighted
        current = sum(c * (volts * sums[c] - weighted[c]) for c in sums)
        pots[step + 1, x] = volts + sigma * flux - current

    def first_moments(part, x, _):
        later = moments[0, x] if part else 0.0
        later_weighted = moments[1, x] if part else 0.0
        for j in range(part * CHUNK, (part + 1) * CHUNK):
            share = state[1 + j, x] * float(gate_conduct[j] * gate_decay[j])
            later += share
            later_weighted += share * float(gate_reversal[j])
        moments[0, x] = later
        moments[1, x] = later_weighted
        return 0

    def send_edges(phase):
        step = WIDE * phase
        for side in range(2):
            out_x[phase, side, 0] = pots[step, ends_x[side]]
            for x in range(nx):
                y = ends_y[side]
                out_y[phase, side, 0, x : x + 1, :] = pots[step, x, y : y + 1, :]
        parts = place_.edges(phase, out_x, out_y, in_x, in_y, 0, 1)
        copies = place_.exchange(phase, list(enumerate(parts)), send_sem, recv_sem)
        start(copies)
        return copies

    def send_rest(phase):
        step = WIDE * phase
        for side in range(2):
            x = ends_x[side]
            out_x[phase, side, 1] = pots[step, x + 1 - 2 * side]
            out_x[phase, side, 2] = moments[0, x]
            out_x[phase, side, 3] = moments[1, x]
            if phase == 0:
                out_x[phase, side, 4] = state[GATES + 1, x]
            for j, y in enumerate(ends_y):
                out_c[phase, 2 * side + j] = pots[step, x, y : y + 1, :]
        for x in range(nx):
            for side, y in enumerate(ends_y):
                inward = y + 1 - 2 * side
                rows = [pots[step, x, inward : inward + 1, :]]
                rows += [moments[f, x, y : y + 1, :] for f in range(2)]
                if phase == 0:
                    rows.append(state[GATES + 1, x, y : y + 1, :])
                for f, row in enumerate(rows):
                    out_y[phase, side, 1 + f, x : x + 1, :] = row
        parts = place_.edges(phase, out_x, out_y, in_x, in_y, 1, 4 if phase == 0 else 3)
        parts += place_.corners(phase, out_c, in_c)
        copies = place_.exchange(phase, list(enumerate(parts, 4)), send_sem, recv_sem)
        start(copies)
        return copies

    def correct(step, planes, rows):
        for side, x in enumerate(ends_x):
            beyond = jnp.where(place_.exists[0][side], planes[side][...] - pots[step, x], 0.0)
            pots[step + 1, x] += 0.12 * state[GATES + 1, x] * beyond
        for x in range(nx):
            volts = pots[step, x]
            beyond = jnp.where(low_y, rows[0][x : x + 1, :] - volts, 0.0)
            beyond += jnp.where(high_y, rows[1][x : x + 1, :] - volts, 0.0)
            pots[step + 1, x] += 0.04 * state[GATES + 1, x] * beyond

    def step_ring(phase):
        step = WIDE * phase
        for axis, (into, across, along) in enumerate(((in_x, 0.12, 0.04), (in_y, 0.04, 0.12))):
            for side in range(2):
                volts, far = into[phase, side, 0], into[phase, side, 1]
                near = pots[step, ends_x[side]] if axis == 0 else out_y[phase, side, 0]
                tips = []
                for end in range(2):
                    corner = in_c[phase, 2 * side + end if axis == 0 else 2 * end + side]
                    own = volts[ends_y[end] : ends_y[end] + 1]
                    tips.append(jnp.where(place_.exists[1 - axis][end], corner, own))
                flux = across * (near + far - 2.0 * volts)
                flux += along * (place_.beside_lines(volts, *tips) - 2.0 * volts)
                flux += 0.04 * (place_.beside_z(volts, volts, volts) - 2.0 * volts)
                gain = np.float64(0.5) * gate_conduct * (1.0 - gate_decay)
                drawn, weighted = 0.0, 0.0
                for j, bend in bends(volts):
                    drawn += bend * float(gain[j])
                    weighted += bend * float(gain[j] * gate_reversal[j])
                drawn += into[phase, side, 2] + float(gain.sum())
                weighted += into[phase, side, 3] + float((gain * gate_reversal).sum())
                fresh = volts + in_sigma(axis, side) * flux - (volts * drawn - weighted)
                ring[phase, 2 * axis + side] = fresh

    def in_sigma(axis, side):
        return (in_x, in_y)[axis][0, side, 4]

    def to_all(src, dst, which):
        def send(i, _):
            there = place_.ring_size * lax.rem(i, N_RING) + i // N_RING
            pltpu.make_async_remote_copy(
                src_ref=src.at[there], dst_ref=dst.at[slab], send_sem=row_sem.at[which, 0],
                recv_sem=row_sem.at[which, 1], device_id=(1, there, col), device_id_type=MESH,
            ).start()
            return 0

        lax.fori_loop(0, n_slab, send, 0)

    def heart():
        loads = [
            load(vol.at[0, 0], pots.at[0], send_sem.at[4]),
        ]
        for part in range(PARTS):
            rows = pl.ds(1 + part * CHUNK, CHUNK + part // (PARTS - 1))
            loads.append(load(vol.at[0, rows], state.at[rows], send_sem.at[5 + part]))
        metas = [
            load(src.at[0], meta.at[i], meta_sem.at[i])
            for i, src in enumerate((line_hbm, dest_hbm, target_hbm))
        ]
        place_.greet(last=place_.across(1))
        loads[0].wait()
        place_.await_met()
        edges = send_edges(0)
        for part in range(PARTS):
            loads[1 + part].wait()
            lax.fori_loop(0, nx, functools.partial(first_moments, part), 0, unroll=2)
        rest = send_rest(0)

        for copy in metas:
            copy.wait()
        lines = nx * ny
        fill_picks(lines)
        for phase in range(PHASES):
            step = WIDE * phase

            def first(x, _):
                step_plane(step, x, False)
                return 0

            def second(x, _):
                step_plane(step + 1, x, phase + 1 < PHASES)
                return 0

            lax.fori_loop(0, nx, first, 0, unroll=2)
            if phase + 1 == PHASES:
                pl.semaphore_wait(ready_sem, N_RING)
                to_all(lines_out, lines_in, 1)
            wait_recv(edges)
            correct(
                step, [in_x.at[phase, side, 0] for side in range(2)],
                [in_y.at[phase, side, 0] for side in range(2)],
            )
            lax.fori_loop(0, nx, second, 0, unroll=2)
            wait_recv(rest)
            step_ring(phase)
            correct(
                step + 1, [ring.at[phase, side] for side in range(2)],
                [ring.at[phase, 2 + side] for side in range(2)],
            )
            if phase + 1 < PHASES:
                wait_send(edges + rest)
                edges = send_edges(phase + 1)
                rest = send_rest(phase + 1)

        state[0] = pots[STEPS]
        final = pots[STEPS].reshape(lines, nz)
        source = jnp.concatenate([final[:, :LANES], final[:, LANES:]], axis=0)
        rows = matmul(picks[...], split_halves(source), ((1,), (0,)))
        rows_out[...] = rows.reshape(n_slab, 4, LANES)
        to_all(rows_out, rows_in, 0)
        wait_whole(rows_out, row_sem.at[0, 0])
        wait_whole(lines_out, row_sem.at[1, 0])
        wait_send(edges + rest)

    def fill_picks(lines):
        epi = meta.shape[2]
        line, dest, target = meta[0], meta[1], meta[2]
        slots = 4 * n_slab
        own = iota((slots, epi), 0)
        marks = own // 4 == dest
        before = (iota((epi, epi), 0) < iota((epi, epi), 1)).astype(jnp.bfloat16)
        rank = matmul(marks.astype(jnp.float32).astype(jnp.bfloat16), before, ((1,), (0,)))
        wanted = ((own // 2) % 2).astype(jnp.float32)
        place = jnp.logical_and(marks, rank == wanted)
        half = (own % 2).astype(jnp.float32)
        place = place.astype(jnp.float32)
        places = jnp.concatenate([place * (1.0 - half), place * half], axis=1)
        held = (iota((lines, epi), 0) == line).astype(jnp.float32).astype(jnp.bfloat16)
        for h in range(2):
            part = matmul(
                places[:, h * epi : (h + 1) * epi].astype(jnp.bfloat16), held, ((1,), (1,))
            ).astype(jnp.bfloat16)
            picks[:, h * lines : (h + 1) * lines] = part
            picks[:, (h + 2) * lines : (h + 3) * lines] = part
        own_d = iota((n_slab, epi), 0)
        marks_d = own_d == dest
        rank_d = matmul(marks_d.astype(jnp.float32).astype(jnp.bfloat16), before, ((1,), (0,)))
        goals = []
        for r in range(CAP):
            chosen = jnp.logical_and(marks_d, rank_d == float(r))
            goal = jnp.where(chosen, (target + 1).astype(jnp.float32), 0.0)
            goals.append(jnp.sum(goal, axis=1, keepdims=True) - 1.0)
        lines_out[:, 0, :] = jnp.where(iota((n_slab, NARROW), 1) == 0, goals[0], goals[1])

    heart()


def torso_part(
    place_, vol, out, rows_in, hits_ref, lines_in,
    pots, coef, drive, out_x, out_y, out_c, in_x, in_y, in_c, ring_x, ring_y,
    send_sem, recv_sem, row_sem, ready_sem,
):
    n_slab, slab, col = place_.n_slab, place_.slab, place_.col
    low_y, high_y = place_.low_y, place_.high_y
    nx, ny, nz = vol.shape[2:]
    tx = SEGMENTS * nx
    ends = ((0, 0), (SEGMENTS - 1, nx - 1))
    before_last = 1.0 - relax_omega

    def field(f):
        return vol.at[0, pl.ds(SEGMENTS * f, SEGMENTS)]

    def before(step):
        return pots.at[step - 1] if step else out.at[1]

    def coefficients(k, _):
        for r in range(nx):
            gain = relax_omega / (6.0 + out[2, k, r])
            coef[k, r] = gain
            drive[k, r] = gain * drive[k, r]
        return 0

    def send_edges(phase):
        step = WIDE * phase
        for side, (k, r) in enumerate(ends):
            out_x[phase, side, 0] = pots[step, k, r]

        def pack(k, _):
            for r in range(nx):
                for side, y in enumerate((0, ny - 1)):
                    row = pots[step, k, r, y : y + 1, :]
                    out_y[phase, side, 0, pl.ds(k * nx + r, 1), :] = row
            return 0

        lax.fori_loop(0, SEGMENTS, pack, 0)
        parts = place_.edges(phase, out_x, out_y, in_x, in_y, 0, 1)
        copies = place_.exchange(phase, list(enumerate(parts)), send_sem, recv_sem)
        start(copies)
        return copies

    def send_rest(phase):
        step = WIDE * phase
        old = before(step)
        for side, (k, r) in enumerate(ends):
            out_x[phase, side, 1] = pots[step, k, r + 1 - 2 * side]
            out_x[phase, side, 2] = before_last * old[k, r] + drive[k, r]
            if phase == 0:
                out_x[phase, side, 3] = coef[k, r]
            for j, y in enumerate((0, ny - 1)):
                out_c[phase, 2 * side + j] = pots[step, k, r, y : y + 1, :]

        def pack(k, _):
            for r in range(nx):
                added = before_last * old[k, r] + drive[k, r]
                for side, y in enumerate((0, ny - 1)):
                    inward = y + 1 - 2 * side
                    rows = [pots[step, k, r, inward : inward + 1, :], added[y : y + 1]]
                    if phase == 0:
                        rows.append(coef[k, r, y : y + 1, :])
                    for f, row in enumerate(rows):
                        out_y[phase, side, 1 + f, pl.ds(k * nx + r, 1), :] = row
            return 0

        lax.fori_loop(0, SEGMENTS, pack, 0)
        parts = place_.edges(phase, out_x, out_y, in_x, in_y, 1, 3 if phase == 0 else 2)
        parts += place_.corners(phase, out_c, in_c)
        copies = place_.exchange(phase, list(enumerate(parts, 4)), send_sem, recv_sem)
        start(copies)
        return copies

    def sweep(step):
        old = before(step)

        def segment(k, _):
            planes = [pots[step, k, r] for r in range(nx)]
            below = jnp.where(k > 0, pots[step, jnp.maximum(k - 1, 0), nx - 1], 0.0)
            above = jnp.where(
                k < SEGMENTS - 1, pots[step, jnp.minimum(k + 1, SEGMENTS - 1), 0], 0.0
            )
            around = [below] + planes + [above]
            for r in range(nx):
                beside = around[r] + around[r + 2]
                beside += place_.beside_lines(planes[r], 0.0, 0.0)
                beside += place_.beside_z(planes[r], 0.0, 0.0)
                pots[step + 1, k, r] = drive[k, r] + before_last * old[k, r] + coef[k, r] * beside
            return 0

        lax.fori_loop(0, SEGMENTS, segment, 0)

    def correct(step, planes, rows):
        for side, (k, r) in enumerate(ends):
            beyond = jnp.where(place_.exists[0][side], planes[side][...], 0.0)
            pots[step + 1, k, r] += coef[k, r] * beyond

        def segment(k, _):
            low, high = (face[pl.ds(k * nx, nx), :] for face in rows)
            for r in range(nx):
                beyond = jnp.where(low_y, low[r : r + 1], 0.0)
                beyond += jnp.where(high_y, high[r : r + 1], 0.0)
                fresh = pots[step + 1, k, r] + coef[k, r] * beyond
                pots[step + 1, k, r] = fresh
                if step + 2 == STEPS:
                    out[1, k, r] = fresh
                if step + 1 == STEPS:
                    out[0, k, r] = fresh
            return 0

        lax.fori_loop(0, SEGMENTS, segment, 0)

    def step_ring(phase):
        step = WIDE * phase
        for side in range(2):
            cells = in_x[phase, side, 0]
            tips = [
                jnp.where(place_.exists[1][end], in_c[phase, 2 * side + end], 0.0)
                for end in range(2)
            ]
            beside = pots[step, *ends[side]] + in_x[phase, side, 1]
            beside += place_.beside_lines(cells, *tips) + place_.beside_z(cells, 0.0, 0.0)
            ring_x[phase, side] = in_x[phase, side, 2] + in_x[0, side, 3] * beside
        for side in range(2):
            tips = [
                jnp.where(place_.exists[0][end], in_c[phase, 2 * end + side], 0.0)
                for end in range(2)
            ]
            for k in range(SEGMENTS):
                rows = pl.ds(k * nx, nx)
                cells = in_y[phase, side, 0, rows, :]
                low = in_y[phase, side, 0, k * nx - 1 : k * nx, :] if k else tips[0]
                high = tips[1]
                if k + 1 < SEGMENTS:
                    high = in_y[phase, side, 0, (k + 1) * nx : (k + 1) * nx + 1, :]
                beside = out_y[phase, side, 0, rows, :] + in_y[phase, side, 1, rows, :]
                beside += place_.beside_lines(cells, low, high) + place_.beside_z(cells, 0.0, 0.0)
                ring_y[phase, side, rows, :] = (
                    in_y[phase, side, 2, rows, :] + in_y[0, side, 3, rows, :] * beside
                )

    def torso():
        loads = [
            load(field(0), pots.at[0], send_sem.at[4]),
            load(field(2), out.at[2], send_sem.at[5]),
            load(field(3), drive, send_sem.at[6]),
            load(field(1), out.at[1], send_sem.at[7]),
        ]
        ring_size = place_.ring_size
        at = lax.rem(slab, ring_size)

        def along(k):
            return (1, slab - at + lax.rem(at + k + ring_size, ring_size), col)

        others = []
        if ring_size > 2:
            others += [(at == 0, along(-1)), (at == ring_size - 1, along(1))]
        for k in sorted(range(2, ring_size - 1), key=lambda k: -min(k, ring_size - k)):
            others.append((slab >= 0, along(k)))
        place_.greet(first=others)

        hearts = place_.across(0)
        place_.await_met(others + hearts)
        for _, there in hearts:
            pl.semaphore_signal(ready_sem, inc=1, device_id=there, device_id_type=MESH)
        loads[0].wait()
        edges = send_edges(0)
        for copy in loads[1:]:
            copy.wait()
        lax.fori_loop(0, SEGMENTS, coefficients, 0)
        rest = send_rest(0)
        for phase in range(PHASES):
            step = WIDE * phase
            sweep(step)
            wait_recv(edges)
            correct(
                step, [in_x.at[phase, side, 0] for side in range(2)],
                [in_y.at[phase, side, 0] for side in range(2)],
            )
            sweep(step + 1)
            wait_recv(rest)
            step_ring(phase)
            correct(
                step + 1, [ring_x.at[phase, side] for side in range(2)],
                [ring_y.at[phase, side] for side in range(2)],
            )
            if phase + 1 < PHASES:
                wait_send(edges + rest)
                edges = send_edges(phase + 1)
                rest = send_rest(phase + 1)

        wait_whole(lines_in, row_sem.at[1, 1])
        slots = (n_slab, CAP * n_slab)
        goal = jnp.where(iota(slots, 1) < n_slab, lines_in[:, 0, 0:1], lines_in[:, 0, 1:2])
        marks = jnp.where(iota(slots, 0) == iota(slots, 1) % n_slab, goal, 0.0)
        marks = jnp.sum(marks, axis=0, keepdims=True)
        goals = iota((tx * ny, CAP * n_slab), 0).astype(jnp.float32)
        hits = (goals == marks).astype(jnp.float32).astype(jnp.bfloat16)
        hits_ref[:, : CAP * n_slab] = hits
        hits_ref[:, CAP * n_slab :] = hits
        wait_whole(rows_in, row_sem.at[0, 1])
        wait_send(edges + rest)

    torso()


def main_kernel(n_slab, n_col, heart_refs, torso_refs, *refs):
    vol, line, dest, target, state, fields, rows_in, hits, lines_in, *scratch = refs
    own_heart, own_torso = scratch[:heart_refs], scratch[heart_refs : heart_refs + torso_refs]
    meta_sem, send_sem, recv_sem, row_sem, ready_sem = scratch[heart_refs + torso_refs :]
    place_ = Place(n_slab, n_col, vol.shape)

    @pl.when(place_.sec == 0)
    def _():
        heart_part(
            place_, vol, line, dest, target, state, rows_in, lines_in, *own_heart,
            meta_sem, send_sem, recv_sem, row_sem, ready_sem,
        )

    @pl.when(place_.sec == 1)
    def _():
        torso_part(
            place_, vol, fields, rows_in, hits, lines_in, *own_torso,
            send_sem, recv_sem, row_sem, ready_sem,
        )


def result_kernel(state, fields, rows, hits, out, inflow_ref, sems):
    nx, ny, nz = state.shape[1:]
    tx = SEGMENTS * nx
    sec = lax.axis_index("sec")

    def heart():
        load(state, out.at[0], sems.at[0]).wait()

    def torso():
        copies = [
            load(fields.at[f], out.at[0, pl.ds(SEGMENTS * f, SEGMENTS)], sems.at[f])
            for f in range(3)
        ]
        got = jnp.concatenate(
            [
                jnp.concatenate([rows[:, 2 * r + h, :] for r in range(CAP)], axis=0)
                for h in range(2)
            ],
            axis=1,
        )
        inflow = matmul(hits[...], split_halves(got), ((1,), (0,)))
        inflow_ref[...] = inflow.reshape(SEGMENTS, nx, ny, nz)
        copies.append(load(inflow_ref, out.at[0, pl.ds(3 * SEGMENTS, SEGMENTS)], sems.at[3]))
        for copy in copies:
            copy.wait()

    pl.when(sec == 0)(heart)
    pl.when(sec == 1)(torso)


def solution(mesh):
    n_slab, n_col = mesh.shape["slab"], mesh.shape["col"]

    def on_device(volume, epi_line, epi_dest, epi_target):
        _, fields, nx, ny, nz = volume.shape
        epi = epi_line.shape[-1]
        tx = SEGMENTS * nx
        f32, dma = jnp.float32, pltpu.SemaphoreType.DMA
        volume, epi_line, epi_dest, epi_target = (
            pltpu.with_memory_space_constraint(x, pltpu.HBM)
            for x in (volume, epi_line, epi_dest.reshape(epi_line.shape), epi_target)
        )
        hbm = pl.BlockSpec(memory_space=pltpu.HBM)
        vmem = pl.BlockSpec(memory_space=pltpu.VMEM)
        heart_scratch = [
                pltpu.VMEM((STEPS + 1, nx, ny, nz), f32),
                pltpu.VMEM((2, nx, ny, nz), f32),
                pltpu.VMEM((PHASES, 2, 5, ny, nz), f32),
                pltpu.VMEM((PHASES, 2, 5, nx, nz), f32),
                pltpu.VMEM((PHASES, 4, 1, nz), f32),
                pltpu.VMEM((PHASES, 2, 5, ny, nz), f32),
                pltpu.VMEM((PHASES, 2, 5, nx, nz), f32),
                pltpu.VMEM((PHASES, 4, 1, nz), f32),
                pltpu.VMEM((PHASES, 4, ny, nz), f32),
                pltpu.VMEM((4 * n_slab, 4 * nx * ny), jnp.bfloat16),
                pltpu.VMEM((3, 1, epi), jnp.int32),
                pltpu.VMEM((n_slab, 4, LANES), f32),
                pltpu.VMEM((n_slab, 1, NARROW), f32),
        ]
        torso_scratch = [
                pltpu.VMEM((STEPS + 1, SEGMENTS, nx, ny, nz), f32),
                pltpu.VMEM((SEGMENTS, nx, ny, nz), f32),
                pltpu.VMEM((SEGMENTS, nx, ny, nz), f32),
                pltpu.VMEM((PHASES, 2, 4, ny, nz), f32),
                pltpu.VMEM((PHASES, 2, 4, tx, nz), f32),
                pltpu.VMEM((PHASES, 4, 1, nz), f32),
                pltpu.VMEM((PHASES, 2, 4, ny, nz), f32),
                pltpu.VMEM((PHASES, 2, 4, tx, nz), f32),
                pltpu.VMEM((PHASES, 4, 1, nz), f32),
                pltpu.VMEM((PHASES, 2, ny, nz), f32),
                pltpu.VMEM((PHASES, 2, tx, nz), f32),
        ]
        regular = pltpu.SemaphoreType.REGULAR
        state, fields, rows, hits = pl.pallas_call(
            functools.partial(
                main_kernel, n_slab, n_col, len(heart_scratch), len(torso_scratch)
            ),
            out_shape=(
                jax.ShapeDtypeStruct((fields, nx, ny, nz), f32),
                jax.ShapeDtypeStruct((3, SEGMENTS, nx, ny, nz), f32),
                jax.ShapeDtypeStruct((n_slab, 4, LANES), f32),
                jax.ShapeDtypeStruct((tx * ny, 2 * CAP * n_slab), jnp.bfloat16),
            ),
            in_specs=[hbm] * 4,
            out_specs=(vmem,) * 4,
            scratch_shapes=[
                pltpu.VMEM((n_slab, 1, NARROW), f32),
                *heart_scratch, *torso_scratch,
                dma((3,)), dma((12,)), dma((PHASES, 12)), dma((2, 2)), regular,
            ],
            compiler_params=pltpu.CompilerParams(
                collective_id=0, has_side_effects=True, vmem_limit_bytes=VMEM_LIMIT
            ),
        )(volume, epi_line, epi_dest, epi_target)
        return pl.pallas_call(
            result_kernel,
            out_shape=jax.ShapeDtypeStruct(volume.shape, f32),
            in_specs=[vmem, vmem, vmem, vmem],
            out_specs=hbm,
            scratch_shapes=[pltpu.VMEM((SEGMENTS, nx, ny, nz), f32), dma((4,))],
            compiler_params=pltpu.CompilerParams(vmem_limit_bytes=VMEM_LIMIT),
        )(state, fields, rows, hits)

    return jax.shard_map(
        on_device,
        mesh=mesh,
        in_specs=(
            P("sec", None, "slab", "col", None),
            P("slab", "col", None),
            P("slab", "col", None, None),
            P("slab", "col", None),
        ),
        out_specs=P("sec", None, "slab", "col", None),
        check_vma=False,
    )
```
